512 devices in a mesh: member: 16 (over y, core), dom: 32 (over z, x).
Axes of the slice: x: 4, y: 8, z: 8, core: 2. Of those that a mesh axis runs over, the one named last changes fastest.
Arguments:
- grid_in: bfloat16 [524288, 227], P(('member', 'dom')), parts along dimension 0, may hold values from -6 to 6
- w_embed: bfloat16 [227, 512], replicated, may hold values from -0.375 to 0.375
- w_grid_send: bfloat16 [512, 512], replicated, may hold values from -0.25 to 0.25
- enc_feat: bfloat16 [4, 65536], P(None, 'dom'), may hold values from -6 to 6
- w_enc_edge: bfloat16 [4, 512], replicated, may hold values from -3 to 3
- enc_sender: int32 [65536], P('dom'), may hold values from 0 to 1535, as said below
- enc_offset: int32 [65536], P('dom'), may hold values from -1 to 127, as said below
- grid_rows: int32 [1024, 16], P('dom'), may hold values from 0 to 1023, as said below
- w_proc_send: bfloat16 [2, 512, 512], replicated, may hold values from -0.25 to 0.25
- w_proc_edge: bfloat16 [2, 4, 512], replicated, may hold values from -3 to 3
- w_proc_node: bfloat16 [2, 512, 512], replicated, may hold values from -0.25 to 0.25
- mesh_feat: bfloat16 [4, 32768], P(None, 'dom'), may hold values from -6 to 6
- mesh_sender: int32 [32768], P('dom'), may hold values from 0 to 383, as said below
- mesh_offset: int32 [32768], P('dom'), may hold values from -1 to 127, as said below
- mesh_rows: int32 [1024, 8], P('dom'), may hold values from 0 to 127, as said below
- w_skip: bfloat16 [512, 512], replicated, may hold values from -0.25 to 0.25
- w_dec: bfloat16 [512, 512], replicated, may hold values from -0.25 to 0.25
- w_dec_edge: bfloat16 [4, 512], replicated, may hold values from -3 to 3
- dec_feat: bfloat16 [4, 98304], P(None, 'dom'), may hold values from -6 to 6
- dec_sender: int32 [98304], P('dom'), may hold values from 0 to 383, as said below
- dec_offset: int32 [98304], P('dom'), may hold values from -1 to 127, as said below
- dec_block: int32 [768], P('dom'), may hold values from 0 to 7, as said below
- dec_rows: int32 [1024, 8], P('dom'), may hold values from 0 to 127, as said below
- w_out: bfloat16 [512, 227], replicated, may hold values from -0.25 to 0.25
Outputs:
- forecast: bfloat16 [524288, 227], P(('member', 'dom')), parts along dimension 0
The draws below stay inside these ranges and needn't reach their ends.
There are 16 independent parts, one for each index of `member`. The reference program is written for one: setup_inputs(seed, part) draws one part's arguments, and reference() takes and returns one part's arrays. A program takes and returns all parts, laid end to end along the dimension named above; an argument that names none is the same for every part. Nothing has to cross between parts.
Inputs may be any that keep to these rules, and one draw needn't show every extreme that they name: `enc_sender`: an entry below 1024 is a grid row of the device that holds the edge; an entry 1024 + p * 16 + s names slot s of what device p lends it, never the device itself. `enc_offset`: A mesh row of the holding device; -1 marks a padded edge. `grid_rows`: row d * 32 + p holds the local grid rows of device p that p lends to device d. `mesh_sender`: an entry below 128 is a mesh row of the holding device; an entry 128 + p * 8 + s names slot s of what device p lends it, never the device itself. `mesh_offset`: A mesh row of the holding device; -1 marks a padded edge. `mesh_rows`: row d * 32 + p holds the local mesh rows of device p that p lends to device d. `dec_sender`: an entry below 128 is a mesh row of the holding device; an entry 128 + p * 8 + s names slot s of what device p lends it, never the device itself. `dec_offset`: A row inside the 128-row grid block named by dec_block; -1 marks a padded edge. `dec_block`: A 128-row block of the holding device's grid rows. `dec_rows`: row d * 32 + p holds the local mesh rows of device p that p lends to device d.
All inputs are finite; a program needn't handle non-finite values.
Results may differ from the reference program's by a relative error of at most 0.012.
Values may be sent and summed in bfloat16 or wider, within the bound.
A program may use at most 64 MiB of HBM per device.

```python
import jax
import jax.numpy as jnp

D = 512
CH = 227
EF = 4
G_DEV = 1024
M_DEV = 128
LAYERS = 2
SLOTS_GRID = 16
SLOTS_MESH = 8
SLOTS_DEC = 8
BLK_ENC = 16
BLK_MESH = 8
BLK_DEC = 24
GRID = 32768
MESH = 4096
ENC_EDGES = 65536
MESH_EDGES = 32768
DEC_EDGES = 98304
N_DOM = 32


def edge_lists(key, n_local, slots, edges_dev, n_recv):
    subkeys = jax.random.split(key, 6)
    edge_shape = (N_DOM, edges_dev)
    device = jnp.arange(N_DOM, dtype=jnp.int32)[:, None]
    remote = jax.random.randint(subkeys[0], edge_shape, 0, 4) == 0
    local_row = jax.random.randint(subkeys[1], edge_shape, 0, n_local)
    peer_index = (device + 1 + jax.random.randint(subkeys[2], edge_shape, 0, N_DOM - 1)) % N_DOM
    slot_pick = jax.random.randint(subkeys[3], edge_shape, 0, slots)
    senders = jnp.where(remote, n_local + peer_index * slots + slot_pick, local_row)
    senders = senders.at[0, 0].set(n_local + (N_DOM - 1) * slots + slots - 1).at[0, 1].set(0)
    targets = jax.random.randint(subkeys[4], edge_shape, 0, n_recv)
    is_live = jax.random.randint(subkeys[5], edge_shape, 0, 8) < 7
    targets = jnp.where(is_live, targets, -1)
    targets = targets.at[0, 2].set(-1).at[0, 3].set(n_recv - 1)
    return (senders.reshape(-1).astype(jnp.int32), targets.reshape(-1).astype(jnp.int32))


def lend_table(key, slots, n_local):
    listed = jax.random.randint(key, (N_DOM * N_DOM, slots), 0, n_local)
    return listed.at[0, 0].set(0).at[0, 1].set(n_local - 1).astype(jnp.int32)


def draw_enc_sender(key, part):
    return edge_lists(jax.random.fold_in(key, 11), G_DEV, SLOTS_GRID, BLK_ENC * 128, M_DEV)[0]


def draw_enc_offset(key, part):
    return edge_lists(jax.random.fold_in(key, 11), G_DEV, SLOTS_GRID, BLK_ENC * 128, M_DEV)[1]


def draw_mesh_sender(key, part):
    return edge_lists(jax.random.fold_in(key, 12), M_DEV, SLOTS_MESH, BLK_MESH * 128, M_DEV)[0]


def draw_mesh_offset(key, part):
    return edge_lists(jax.random.fold_in(key, 12), M_DEV, SLOTS_MESH, BLK_MESH * 128, M_DEV)[1]


def draw_dec_sender(key, part):
    return edge_lists(jax.random.fold_in(key, 13), M_DEV, SLOTS_DEC, BLK_DEC * 128, 128)[0]


def draw_dec_offset(key, part):
    return edge_lists(jax.random.fold_in(key, 13), M_DEV, SLOTS_DEC, BLK_DEC * 128, 128)[1]


def draw_grid_rows(key, part):
    key = jax.random.fold_in(key, 21)
    return lend_table(key, SLOTS_GRID, G_DEV)


def draw_mesh_rows(key, part):
    key = jax.random.fold_in(key, 22)
    return lend_table(key, SLOTS_MESH, M_DEV)


def draw_dec_rows(key, part):
    key = jax.random.fold_in(key, 23)
    return lend_table(key, SLOTS_DEC, M_DEV)


def draw_dec_block(key, part):
    key = jax.random.fold_in(key, 31)
    blocks = jax.random.randint(key, (N_DOM * BLK_DEC,), 0, G_DEV // 128)
    return blocks.at[0].set(0).at[1].set(G_DEV // 128 - 1).astype(jnp.int32)


def steps_of(own_key, extent, cuts, least, largest):
    gain, own = 1.0, jax.random.fold_in(own_key, 6)
    for dim, shards_of in cuts:
        draws = jnp.exp(jax.random.uniform(jax.random.fold_in(own, dim), (shards_of,), jnp.float32, least / len(cuts), largest / len(cuts)))
        gain = gain * jnp.repeat(draws, extent[dim] // shards_of).reshape([-1 if axis == dim else 1 for axis in range(len(extent))])
    return gain


def centred(rng, shape, deviation, most, pieces=(), kind=jnp.bfloat16):
    drawn = jax.random.normal(rng, shape, jnp.float32) * deviation
    if len(pieces) > 0:
        drawn = steps_of(rng, shape, pieces, -0.22, 0.18) * drawn
    return jnp.clip(drawn, min=-most, max=most).astype(kind)


def setup_inputs(seed: int = 0, part: int = 0) -> dict:
    streams_of = jax.random.split(jax.random.key(seed), 25)
    part_keys = jax.random.split(jax.random.fold_in(streams_of[24], part), 25)
    return {
        "grid_in": centred(part_keys[0], (GRID, CH), 1.0, 6.0, ((0, 32),)),
        "w_embed": centred(streams_of[1], (CH, D), CH ** -0.5, 0.375),
        "w_grid_send": centred(streams_of[2], (D, D), D ** -0.5, 0.25),
        "enc_feat": centred(streams_of[3], (EF, ENC_EDGES), 1.0, 6.0, ((1, 32),)),
        "w_enc_edge": centred(streams_of[4], (EF, D), EF ** -0.5, 3.0),
        "enc_sender": draw_enc_sender(jax.random.fold_in(streams_of[24], 71), part),
        "enc_offset": draw_enc_offset(jax.random.fold_in(streams_of[24], 71), part),
        "grid_rows": draw_grid_rows(jax.random.fold_in(streams_of[24], 71), part),
        "w_proc_send": centred(streams_of[8], (LAYERS, D, D), D ** -0.5, 0.25),
        "w_proc_edge": centred(streams_of[9], (LAYERS, EF, D), EF ** -0.5, 3.0),
        "w_proc_node": centred(streams_of[10], (LAYERS, D, D), D ** -0.5, 0.25),
        "mesh_feat": centred(streams_of[11], (EF, MESH_EDGES), 1.0, 6.0, ((1, 32),)),
        "mesh_sender": draw_mesh_sender(jax.random.fold_in(streams_of[24], 71), part),
        "mesh_offset": draw_mesh_offset(jax.random.fold_in(streams_of[24], 71), part),
        "mesh_rows": draw_mesh_rows(jax.random.fold_in(streams_of[24], 71), part),
        "w_skip": centred(streams_of[15], (D, D), D ** -0.5, 0.25),
        "w_dec": centred(streams_of[16], (D, D), D ** -0.5, 0.25),
        "w_dec_edge": centred(streams_of[17], (EF, D), EF ** -0.5, 3.0),
        "dec_feat": centred(streams_of[18], (EF, DEC_EDGES), 1.0, 6.0, ((1, 32),)),
        "dec_sender": draw_dec_sender(jax.random.fold_in(streams_of[24], 71), part),
        "dec_offset": draw_dec_offset(jax.random.fold_in(streams_of[24], 71), part),
        "dec_block": draw_dec_block(jax.random.fold_in(streams_of[24], 71), part),
        "dec_rows": draw_dec_rows(jax.random.fold_in(streams_of[24], 71), part),
        "w_out": centred(streams_of[23], (D, CH), D ** -0.5, 0.25),
    }


def source_rows(senders, lent, n_local, edges_dev):
    slots = lent.shape[1]
    edge_index = jnp.arange(senders.shape[0], dtype=jnp.int32)
    device = edge_index // edges_dev
    shifted = jnp.maximum(senders - n_local, 0)
    peer_index = shifted // slots
    slot_index = shifted % slots
    listed = lent[device * N_DOM + peer_index, slot_index]
    return jnp.where(senders >= n_local, peer_index * n_local + listed, device * n_local + senders).astype(jnp.int32)


def edge_messages(picked, features, w_edge):
    edge_term = jnp.dot(features.T, w_edge, preferred_element_type=jnp.float32)
    return jax.nn.silu(picked.astype(jnp.float32) + edge_term).astype(jnp.bfloat16)


def mean_into(messages, targets, n_rows):
    is_live = targets >= 0
    weights = is_live.astype(jnp.float32)
    safe = jnp.where(is_live, targets, 0).astype(jnp.int32)
    summed = jax.ops.segment_sum(messages.astype(jnp.float32) * weights[:, None], safe, num_segments=n_rows)
    counted = jax.ops.segment_sum(weights, safe, num_segments=n_rows)
    return (summed / jnp.maximum(counted, 1.0)[:, None]).astype(jnp.bfloat16)


def local_targets(offsets, edges_dev, n_local):
    device = jnp.arange(offsets.shape[0], dtype=jnp.int32) // edges_dev
    return jnp.where(offsets >= 0, device * n_local + offsets, -1).astype(jnp.int32)


def reference(grid_in, w_embed, w_grid_send, enc_feat, w_enc_edge, enc_sender, enc_offset, grid_rows,
              w_proc_send, w_proc_edge, w_proc_node, mesh_feat, mesh_sender, mesh_offset, mesh_rows,
              w_skip, w_dec, w_dec_edge, dec_feat, dec_sender, dec_offset, dec_block, dec_rows, w_out):
    grid_latent = jax.nn.silu(jnp.dot(grid_in, w_embed, preferred_element_type=jnp.float32)).astype(jnp.bfloat16)
    grid_send = jnp.dot(grid_latent, w_grid_send, preferred_element_type=jnp.float32).astype(jnp.bfloat16)
    enc_edges = BLK_ENC * 128
    senders = source_rows(enc_sender, grid_rows, G_DEV, enc_edges)
    messages = edge_messages(grid_send[senders], enc_feat, w_enc_edge)
    mesh_latent = mean_into(messages, local_targets(enc_offset, enc_edges, M_DEV), MESH)
    mesh_edges = BLK_MESH * 128
    senders = source_rows(mesh_sender, mesh_rows, M_DEV, mesh_edges)
    targets = local_targets(mesh_offset, mesh_edges, M_DEV)
    for layer_index in range(LAYERS):
        mesh_send = jnp.dot(mesh_latent, w_proc_send[layer_index], preferred_element_type=jnp.float32).astype(jnp.bfloat16)
        messages = edge_messages(mesh_send[senders], mesh_feat, w_proc_edge[layer_index])
        mesh_mean = mean_into(messages, targets, MESH)
        update = jax.nn.silu(jnp.dot(mesh_mean, w_proc_node[layer_index], preferred_element_type=jnp.float32))
        mesh_latent = (mesh_latent.astype(jnp.float32) + update).astype(jnp.bfloat16)
    dec_edges = BLK_DEC * 128
    senders = source_rows(dec_sender, dec_rows, M_DEV, dec_edges)
    messages = edge_messages(mesh_latent[senders], dec_feat, w_dec_edge)
    edge_index = jnp.arange(dec_offset.shape[0], dtype=jnp.int32)
    device = edge_index // dec_edges
    block_of = dec_block[edge_index // 128]
    targets = jnp.where(dec_offset >= 0, device * G_DEV + block_of * 128 + dec_offset, -1).astype(jnp.int32)
    grid_mean = mean_into(messages, targets, GRID)
    mixed = jnp.dot(grid_mean, w_dec, preferred_element_type=jnp.float32) + jnp.dot(grid_latent, w_skip, preferred_element_type=jnp.float32)
    hidden = jax.nn.silu(mixed).astype(jnp.bfloat16)
    return jnp.dot(hidden, w_out, preferred_element_type=jnp.float32).astype(jnp.bfloat16)
```

```python
import jax
import jax.numpy as jnp
from jax import lax
from jax.experimental import pallas as pl
from jax.experimental.pallas import tpu as pltpu
from jax.sharding import PartitionSpec as P

N_DOM = 32
SLOTS_GRID = 16
SLOTS_MESH = 8
BF = jnp.bfloat16
F32 = jnp.float32


def silu(v):
    half = 0.5 * v
    return half + half * jnp.tanh(half)


def dot(a, b):
    return jnp.dot(a, b, preferred_element_type=F32)


def lanes(shape):
    return lax.broadcasted_iota(jnp.int32, shape, 1).astype(F32)


def rows(shape):
    return lax.broadcasted_iota(jnp.int32, shape, 0).astype(F32)


def hot(index, offset):
    return jnp.where(index == lanes(index.shape) + offset, 1.0, 0.0).astype(BF)


def kernel(
    grid_in,
    w_embed,
    w_grid_send,
    enc_feat,
    w_enc_edge,
    enc_sender,
    enc_offset,
    lists,
    w_proc_send,
    w_proc_edge,
    w_proc_node,
    mesh_feat,
    mesh_sender,
    mesh_offset,
    w_skip,
    w_dec,
    w_dec_edge,
    dec_feat,
    dec_sender,
    dec_target,
    w_out,
    out,
    lists_got,
    grid_out,
    grid_got,
    mesh_out,
    mesh_got,
    lend_grid,
    lend_mesh,
    lend_dec,
    enc_rows,
    mesh_rows,
    dec_rows,
    enc_hot,
    mesh_hot,
    dec_hot,
    enc_to,
    mesh_to,
    dec_to,
    enc_count,
    mesh_count,
    dec_count,
    grid_latent,
    enc_table,
    enc_lent,
    mesh_table,
    enc_sum,
    enc_msg,
    mesh_msg,
    dec_msg,
    mesh_now,
    lists_sem,
    send_sem,
    recv_sem,
):
    me = lax.axis_index("dom")
    width = w_embed.shape[1]
    half = width // 2
    n_grid = grid_in.shape[0]
    n_mesh = mesh_to.shape[0]
    channels = grid_in.shape[1]

    def send_blocks(source, target, size, out_sem, in_sem):
        def step(r, carry):
            pltpu.make_async_remote_copy(
                src_ref=source(r),
                dst_ref=target.at[pl.ds((N_DOM - r) * size, size)],
                send_sem=out_sem,
                recv_sem=in_sem,
                device_id={"dom": lax.rem(me + r, N_DOM)},
                device_id_type=pl.DeviceIdType.MESH,
            ).start()
            return carry

        lax.fori_loop(1, N_DOM, step, 0)

    def wait_for(buffer, size, sem):
        part = buffer.at[pl.ds(size, (N_DOM - 1) * size)]
        pltpu.make_async_copy(part, part, sem).wait()

    barrier = pltpu.get_barrier_semaphore()

    def greet(r, carry):
        pl.semaphore_signal(
            barrier,
            inc=1,
            device_id={"dom": lax.rem(me + r, N_DOM)},
            device_id_type=pl.DeviceIdType.MESH,
        )
        return carry

    lax.fori_loop(1, N_DOM, greet, 0)

    lists_got[0:1] = jnp.zeros((1, 1, 128), jnp.int32)
    grid_got[0:16, :] = jnp.zeros((16, 256), BF)
    for k in range(3):
        mesh_got[k, 0:16, :] = jnp.zeros((16, 256), BF)

    pl.semaphore_wait(barrier, N_DOM - 1)
    send_blocks(
        lambda r: lists.at[pl.ds(lax.rem(me + r, N_DOM), 1)], lists_got, 1, lists_sem.at[0], lists_sem.at[1]
    )

    def embed(i, carry):
        part = pl.ds(pl.multiple_of(i * 256, 256), 256)
        latent = silu(dot(grid_in[part, :], w_embed[...])).astype(BF)
        grid_latent[part, :] = latent
        enc_table[part, :] = dot(latent, w_grid_send[...]).astype(BF)
        return carry

    lax.fori_loop(0, n_grid // 256, embed, 0)

    wait_for(lists_got, 1, lists_sem.at[1])
    listed = lists_got[:, 0, :].astype(F32)
    listed = jnp.transpose(jnp.concatenate([listed, jnp.zeros((96, 128), F32)], axis=0))
    for q in range(N_DOM):
        lend_grid[16 * q : 16 * q + 16, :] = jnp.broadcast_to(listed[0:16, q : q + 1], (16, 128))
        for lent, first in ((lend_mesh, 16), (lend_dec, 24)):
            column = jnp.broadcast_to(listed[first : first + 8, q : q + 1], (8, 128))
            lent[16 * q : 16 * q + 8, :] = column
            lent[16 * q + 8 : 16 * q + 16, :] = column + 128.0

    grid_out[...] = jnp.zeros_like(grid_out)
    for i in range(4):
        part = pl.ds(i * 128, 128)
        picks = jnp.concatenate(
            [hot(lend_grid[part, :], 128.0 * j) for j in range(n_grid // 128)], axis=1
        )
        grid_out[part, 0:channels] = dot(picks, grid_in[...]).astype(BF)
    send_blocks(
        lambda r: grid_out.at[pl.ds(pl.multiple_of(r * 16, 16), 16)],
        grid_got,
        16,
        send_sem.at[0],
        recv_sem.at[0],
    )

    def edge_rows(scratch, feat, sender, n_local, slots):
        edges = sender.shape[1]
        value = sender[...]
        lent = (value - n_local - me * slots) & (N_DOM * slots - 1)
        local = value < n_local
        scratch[...] = jnp.zeros_like(scratch)
        scratch[0:4, :] = feat[...].astype(F32)
        scratch[4:5, :] = jnp.where(local, value, -1).astype(F32)
        scratch[5:6, :] = jnp.where(local, -1, lent).astype(F32)

    def sender_hot(scratch, hots, n_local, n_lent):
        def step(i, carry):
            part = pl.ds(pl.multiple_of(i * 128, 128), 128)
            turned = jnp.transpose(
                jnp.concatenate([scratch[:, part], jnp.zeros((120, 128), F32)], axis=0)
            )
            local = jnp.broadcast_to(turned[:, 4:5], (128, 128))
            lent = jnp.broadcast_to(turned[:, 5:6], (128, 128))
            for j in range(n_local // 128):
                hots[part, 128 * j : 128 * j + 128] = hot(local, 128.0 * j)
            hots[part, n_local : n_local + 128] = turned.astype(BF)
            for j in range(n_lent // 128):
                at = n_local + 128 + 128 * j
                hots[part, at : at + 128] = hot(lent, 128.0 * j)
            return carry

        lax.fori_loop(0, hots.shape[0] // 128, step, 0)

    def receiver_hot(target, hots, count):
        n_rows = hots.shape[0]
        count[...] = jnp.zeros_like(count)

        def step(i, carry):
            part = pl.ds(pl.multiple_of(i * 128, 128), 128)
            wanted = jnp.broadcast_to(target[:, part].astype(F32), (n_rows, 128))
            same = jnp.where(wanted == rows((n_rows, 128)), 1.0, 0.0)
            hots[:, part] = same.astype(BF)
            count[...] += same
            return carry

        lax.fori_loop(0, hots.shape[1] // 128, step, 0)
        total = jnp.sum(count[...], axis=1, keepdims=True)
        count[...] = jnp.broadcast_to(jnp.maximum(total, 1.0), count.shape)

    def edge_weights(table, at, w_edge):
        table[at : at + 128, :] = jnp.zeros((128, width), BF)
        table[at : at + 4, :] = w_edge

    def mean(hots, messages, count):
        return dot(hots, messages) / jnp.concatenate([count] * (width // 128), axis=1)

    edge_rows(enc_rows, enc_feat, enc_sender, n_grid, SLOTS_GRID)
    sender_hot(enc_rows, enc_hot, n_grid, N_DOM * SLOTS_GRID)
    edge_weights(enc_table, n_grid, w_enc_edge[...])

    def enc_local(i, carry):
        part = pl.ds(pl.multiple_of(i * 512, 512), 512)
        enc_sum[part, :] = dot(enc_hot[part, 0 : n_grid + 128], enc_table[...])
        return carry

    lax.fori_loop(0, enc_sum.shape[0] // 512, enc_local, 0)
    receiver_hot(enc_offset, enc_to, enc_count)

    wait_for(grid_got, 16, recv_sem.at[0])

    def embed_lent(i, carry):
        part = pl.ds(pl.multiple_of(i * 256, 256), 256)
        latent = silu(dot(grid_got[part, 0:channels], w_embed[...])).astype(BF)
        enc_lent[part, :] = dot(latent, w_grid_send[...]).astype(BF)
        return carry

    lax.fori_loop(0, enc_lent.shape[0] // 256, embed_lent, 0)

    def enc_remote(i, carry):
        part = pl.ds(pl.multiple_of(i * 512, 512), 512)
        total = enc_sum[part, :] + dot(enc_hot[part, n_grid + 128 :], enc_lent[...])
        enc_msg[part, :] = silu(total).astype(BF)
        return carry

    lax.fori_loop(0, enc_sum.shape[0] // 512, enc_remote, 0)
    mesh_now[...] = mean(enc_to[...], enc_msg[...], enc_count[...]).astype(BF)

    def lend(k, lent, values):
        picks = jnp.concatenate([hot(lent[...], 0.0), hot(lent[...], 128.0)], axis=1)
        stacked = jnp.concatenate([values[:, 0:half], values[:, half:]], axis=0)
        mesh_out[k] = dot(picks, stacked).astype(BF)
        send_blocks(
            lambda r: mesh_out.at[k, pl.ds(pl.multiple_of(r * 16, 16), 16)],
            mesh_got.at[k],
            16,
            send_sem.at[k + 1],
            recv_sem.at[k + 1],
        )

    def borrow(k):
        wait_for(mesh_got.at[k], 16, recv_sem.at[k + 1])
        got = mesh_got[k].astype(F32).reshape(N_DOM, 16, half)
        low = got[:, 0:8, :].reshape(N_DOM * 8, half)
        high = got[:, 8:16, :].reshape(N_DOM * 8, half)
        mesh_table[256:512, :] = jnp.concatenate([low, high], axis=1).astype(BF)

    def messages_of(hots, messages):
        def step(i, carry):
            part = pl.ds(pl.multiple_of(i * 512, 512), 512)
            messages[part, :] = silu(dot(hots[part, :], mesh_table[...])).astype(BF)
            return carry

        lax.fori_loop(0, hots.shape[0] // 512, step, 0)

    for k in range(2):
        values = dot(mesh_now[...], w_proc_send[k]).astype(BF)
        lend(k, lend_mesh, values)
        mesh_table[0:128, :] = values
        edge_weights(mesh_table, 128, w_proc_edge[k])
        if k == 0:
            edge_rows(mesh_rows, mesh_feat, mesh_sender, n_mesh, SLOTS_MESH)
            sender_hot(mesh_rows, mesh_hot, n_mesh, N_DOM * SLOTS_MESH)
            receiver_hot(mesh_offset, mesh_to, mesh_count)
        else:
            edge_rows(dec_rows, dec_feat, dec_sender, n_mesh, SLOTS_MESH)
            sender_hot(dec_rows, dec_hot, n_mesh, N_DOM * SLOTS_MESH)
        borrow(k)
        messages_of(mesh_hot, mesh_msg)
        mesh_mean = mean(mesh_to[...], mesh_msg[...], mesh_count[...]).astype(BF)
        update = silu(dot(mesh_mean, w_proc_node[k]))
        mesh_now[...] = (mesh_now[...].astype(F32) + update).astype(BF)

    lend(2, lend_dec, mesh_now[...])
    mesh_table[0:128, :] = mesh_now[...]
    edge_weights(mesh_table, 128, w_dec_edge[...])
    receiver_hot(dec_target, dec_to, dec_count)
    borrow(2)
    messages_of(dec_hot, dec_msg)

    def decode(i, carry):
        part = pl.ds(pl.multiple_of(i * 256, 256), 256)
        grid_mean = mean(dec_to[part, :], dec_msg[...], dec_count[part, :]).astype(BF)
        mixed = dot(grid_mean, w_dec[...]) + dot(grid_latent[part, :], w_skip[...])
        out[part, :] = dot(silu(mixed).astype(BF), w_out[...]).astype(BF)
        return carry

    lax.fori_loop(0, n_grid // 256, decode, 0)

    wait_for(lists_got, 1, lists_sem.at[0])
    wait_for(grid_out, 16, send_sem.at[0])
    for k in range(3):
        wait_for(mesh_out.at[k], 16, send_sem.at[k + 1])


def local(
    grid_in,
    w_embed,
    w_grid_send,
    enc_feat,
    w_enc_edge,
    enc_sender,
    enc_offset,
    grid_rows,
    w_proc_send,
    w_proc_edge,
    w_proc_node,
    mesh_feat,
    mesh_sender,
    mesh_offset,
    mesh_rows,
    w_skip,
    w_dec,
    w_dec_edge,
    dec_feat,
    dec_sender,
    dec_offset,
    dec_block,
    dec_rows,
    w_out,
):
    n_grid = grid_in.shape[0]
    width = w_embed.shape[1]
    n_mesh = 128
    enc, mesh, dec = enc_sender.shape[0], mesh_sender.shape[0], dec_sender.shape[0]
    lists = jnp.concatenate(
        [grid_rows, mesh_rows, dec_rows, jnp.zeros((N_DOM, 96), jnp.int32)], axis=1
    ).reshape(N_DOM, 1, 128)
    dec_target = jnp.where(
        dec_offset >= 0, jnp.repeat(dec_block * 128, 128) + dec_offset, -1
    )
    operands = (
        grid_in,
        w_embed,
        w_grid_send,
        enc_feat,
        w_enc_edge,
        enc_sender.reshape(1, enc),
        enc_offset.reshape(1, enc),
        lists,
        w_proc_send,
        w_proc_edge,
        w_proc_node,
        mesh_feat,
        mesh_sender.reshape(1, mesh),
        mesh_offset.reshape(1, mesh),
        w_skip,
        w_dec,
        w_dec_edge,
        dec_feat,
        dec_sender.reshape(1, dec),
        dec_target.reshape(1, dec),
        w_out,
    )
    whole = pl.BlockSpec(memory_space=pltpu.VMEM)
    return pl.pallas_call(
        kernel,
        out_shape=jax.ShapeDtypeStruct((n_grid, w_out.shape[1]), BF),
        in_specs=[whole] * len(operands),
        out_specs=whole,
        scratch_shapes=[
            pltpu.VMEM((N_DOM, 1, 128), jnp.int32),
            pltpu.VMEM((512, 256), BF),
            pltpu.VMEM((512, 256), BF),
            pltpu.VMEM((3, 512, 256), BF),
            pltpu.VMEM((3, 512, 256), BF),
            pltpu.VMEM((512, 128), F32),
            pltpu.VMEM((512, 128), F32),
            pltpu.VMEM((512, 128), F32),
            pltpu.VMEM((8, enc), F32),
            pltpu.VMEM((8, mesh), F32),
            pltpu.VMEM((8, dec), F32),
            pltpu.VMEM((enc, n_grid + 128 + 512), BF),
            pltpu.VMEM((mesh, 512), BF),
            pltpu.VMEM((dec, 512), BF),
            pltpu.VMEM((n_mesh, enc), BF),
            pltpu.VMEM((n_mesh, mesh), BF),
            pltpu.VMEM((n_grid, dec), BF),
            pltpu.VMEM((n_mesh, 128), F32),
            pltpu.VMEM((n_mesh, 128), F32),
            pltpu.VMEM((n_grid, 128), F32),
            pltpu.VMEM((n_grid, width), BF),
            pltpu.VMEM((n_grid + 128, width), BF),
            pltpu.VMEM((512, width), BF),
            pltpu.VMEM((512, width), BF),
            pltpu.VMEM((enc, width), F32),
            pltpu.VMEM((enc, width), BF),
            pltpu.VMEM((mesh, width), BF),
            pltpu.VMEM((dec, width), BF),
            pltpu.VMEM((n_mesh, width), BF),
            pltpu.SemaphoreType.DMA((2,)),
            pltpu.SemaphoreType.DMA((4,)),
            pltpu.SemaphoreType.DMA((4,)),
        ],
        compiler_params=pltpu.CompilerParams(
            collective_id=0, has_side_effects=True, vmem_limit_bytes=56 * 1024 * 1024
        ),
        name="graph_weather",
    )(*operands)


def solution(mesh):
    in_specs = (
        P(("member", "dom"), None),
        P(),
        P(),
        P(None, "dom"),
        P(),
        P("dom"),
        P("dom"),
        P("dom", None),
        P(),
        P(),
        P(),
        P(None, "dom"),
        P("dom"),
        P("dom"),
        P("dom", None),
        P(),
        P(),
        P(),
        P(None, "dom"),
        P("dom"),
        P("dom"),
        P("dom"),
        P("dom", None),
        P(),
    )
    out_specs = P(("member", "dom"), None)
    return jax.shard_map(local, mesh=mesh, in_specs=in_specs, out_specs=out_specs, check_vma=False)
```

```python
import jax
import jax.numpy as jnp
from jax import lax
from jax.experimental import pallas as pl
from jax.experimental.pallas import tpu as pltpu
from jax.sharding import PartitionSpec as P

N_DOM = 32
SLOTS_GRID = 16
SLOTS_MESH = 8
BF = jnp.bfloat16
F32 = jnp.float32


def silu(v):
    half = 0.5 * v
    return half + half * jnp.tanh(half)


def dot(a, b):
    return jnp.dot(a, b, preferred_element_type=F32)


def dot_turned(a, b):
    return lax.dot_general(a, b, (((1,), (1,)), ((), ())), preferred_element_type=F32)


def lanes(shape):
    return lax.broadcasted_iota(jnp.int32, shape, 1).astype(F32)


def rows(shape):
    return lax.broadcasted_iota(jnp.int32, shape, 0).astype(F32)


def hot(index, offset):
    return jnp.where(index == lanes(index.shape) + offset, 1.0, 0.0).astype(BF)


def kernel(
    grid_in,
    w_embed,
    w_grid_send,
    enc_feat,
    w_enc_edge,
    enc_sender,
    enc_offset,
    grid_list,
    mesh_list,
    dec_list,
    w_proc_send,
    w_proc_edge,
    w_proc_node,
    mesh_feat,
    mesh_sender,
    mesh_offset,
    w_skip,
    w_dec,
    w_dec_edge,
    dec_feat,
    dec_sender,
    dec_offset,
    dec_block,
    w_out,
    out,
    lists_out,
    lists_got,
    grid_out,
    grid_got,
    mesh_out,
    mesh_got,
    lend_grid,
    lend_mesh,
    lend_dec,
    enc_rows,
    mesh_rows,
    dec_rows,
    enc_hot,
    mesh_hot,
    dec_hot,
    enc_to,
    mesh_to,
    dec_to,
    enc_count,
    mesh_count,
    dec_count,
    grid_latent,
    enc_table,
    enc_lent,
    mesh_table,
    enc_sum,
    enc_msg,
    mesh_msg,
    dec_msg,
    mesh_now,
    grid_turned,
    grid_held,
    w_embed_held,
    w_grid_send_held,
    w_proc_send_held,
    w_proc_node_held,
    w_skip_held,
    w_dec_held,
    w_out_held,
    load_sem,
    lists_sem,
    send_sem,
    recv_sem,
):
    me = lax.axis_index("dom")
    width = w_embed.shape[1]
    half = width // 2
    channels, n_grid = grid_in.shape
    n_mesh = mesh_to.shape[0]

    def send_blocks(source, target, size, out_sem, in_sem):
        def step(r, carry):
            pltpu.make_async_remote_copy(
                src_ref=source(r),
                dst_ref=target.at[pl.ds((N_DOM - r) * size, size)],
                send_sem=out_sem,
                recv_sem=in_sem,
                device_id={"dom": lax.rem(me + r, N_DOM)},
                device_id_type=pl.DeviceIdType.MESH,
            ).start()
            return carry

        lax.fori_loop(1, N_DOM, step, 0)

    def wait_for(buffer, size, sem):
        part = buffer.at[pl.ds(size, (N_DOM - 1) * size)]
        pltpu.make_async_copy(part, part, sem).wait()

    barrier = pltpu.get_barrier_semaphore()

    def greet(r, carry):
        pl.semaphore_signal(
            barrier,
            inc=1,
            device_id={"dom": lax.rem(me + r, N_DOM)},
            device_id_type=pl.DeviceIdType.MESH,
        )
        return carry

    lax.fori_loop(1, N_DOM, greet, 0)

    loads = [
        pltpu.make_async_copy(held_from, held, load_sem.at[i])
        for i, (held_from, held) in enumerate(
            (
                (grid_in, grid_held),
                (w_embed, w_embed_held),
                (w_grid_send, w_grid_send_held),
                (w_proc_send, w_proc_send_held),
                (w_proc_node, w_proc_node_held),
                (w_skip, w_skip_held),
                (w_dec, w_dec_held),
                (w_out, w_out_held),
            )
        )
    ]
    for load in loads:
        load.start()

    slots = jnp.concatenate([grid_list[...], mesh_list[...], dec_list[...]], axis=0).astype(F32)
    slots = jnp.concatenate([slots, jnp.zeros((N_DOM, 96), F32)], axis=1)
    slots = jnp.transpose(jnp.concatenate([slots, jnp.zeros((96, 128), F32)], axis=0))
    for p in range(N_DOM):
        lists_out[p] = slots[p : p + 1, :].astype(jnp.int32)

    lists_got[0:1] = jnp.zeros((1, 1, 128), jnp.int32)
    grid_got[0:16, :] = jnp.zeros((16, 256), BF)
    for k in range(3):
        mesh_got[k, 0:16, :] = jnp.zeros((16, 256), BF)

    pl.semaphore_wait(barrier, N_DOM - 1)
    send_blocks(
        lambda r: lists_out.at[pl.ds(lax.rem(me + r, N_DOM), 1)], lists_got, 1, lists_sem.at[0], lists_sem.at[1]
    )

    loads[0].wait()
    loads[1].wait()
    loads[2].wait()

    def embed(i, carry):
        part = pl.ds(pl.multiple_of(i * 256, 256), 256)
        grid_turned[...] = jnp.transpose(grid_held[:, part])
        latent = silu(dot(grid_turned[...], w_embed_held[...])).astype(BF)
        grid_latent[part, :] = latent
        enc_table[part, :] = dot(latent, w_grid_send_held[...]).astype(BF)
        return carry

    lax.fori_loop(0, n_grid // 256, embed, 0)

    wait_for(lists_got, 1, lists_sem.at[1])
    listed = lists_got[:, 0, :].astype(F32)
    listed = jnp.transpose(jnp.concatenate([listed, jnp.zeros((96, 128), F32)], axis=0))
    for q in range(N_DOM):
        lend_grid[16 * q : 16 * q + 16, :] = jnp.broadcast_to(listed[0:16, q : q + 1], (16, 128))
        for lent, first in ((lend_mesh, 16), (lend_dec, 24)):
            column = jnp.broadcast_to(listed[first : first + 8, q : q + 1], (8, 128))
            lent[16 * q : 16 * q + 8, :] = column
            lent[16 * q + 8 : 16 * q + 16, :] = column + 128.0

    grid_out[...] = jnp.zeros_like(grid_out)
    for i in range(4):
        part = pl.ds(i * 128, 128)
        picks = jnp.concatenate(
            [hot(lend_grid[part, :], 128.0 * j) for j in range(n_grid // 128)], axis=1
        )
        grid_out[part, 0:channels] = dot_turned(picks, grid_held[...]).astype(BF)
    send_blocks(
        lambda r: grid_out.at[pl.ds(pl.multiple_of(r * 16, 16), 16)],
        grid_got,
        16,
        send_sem.at[0],
        recv_sem.at[0],
    )

    def edge_rows(scratch, feat, sender, n_local, slots):
        edges = sender.shape[1]
        value = sender[...]
        lent = (value - n_local - me * slots) & (N_DOM * slots - 1)
        local = value < n_local
        scratch[...] = jnp.zeros_like(scratch)
        scratch[0:4, :] = feat[...].astype(F32)
        scratch[4:5, :] = jnp.where(local, value, -1).astype(F32)
        scratch[5:6, :] = jnp.where(local, -1, lent).astype(F32)

    def sender_hot(scratch, hots, n_local, n_lent):
        def step(i, carry):
            part = pl.ds(pl.multiple_of(i * 128, 128), 128)
            turned = jnp.transpose(
                jnp.concatenate([scratch[:, part], jnp.zeros((120, 128), F32)], axis=0)
            )
            local = jnp.broadcast_to(turned[:, 4:5], (128, 128))
            lent = jnp.broadcast_to(turned[:, 5:6], (128, 128))
            for j in range(n_local // 128):
                hots[part, 128 * j : 128 * j + 128] = hot(local, 128.0 * j)
            hots[part, n_local : n_local + 128] = turned.astype(BF)
            for j in range(n_lent // 128):
                at = n_local + 128 + 128 * j
                hots[part, at : at + 128] = hot(lent, 128.0 * j)
            return carry

        lax.fori_loop(0, hots.shape[0] // 128, step, 0)

    def receiver_hot(target, hots, count, block=None):
        n_rows = hots.shape[0]
        count[...] = jnp.zeros_like(count)

        def step(i, carry):
            part = pl.ds(pl.multiple_of(i * 128, 128), 128)
            wanted = target[:, part]
            if block is not None:
                wanted = jnp.where(wanted >= 0, wanted + 128 * block[0, i], -1)
            wanted = jnp.broadcast_to(wanted.astype(F32), (n_rows, 128))
            same = jnp.where(wanted == rows((n_rows, 128)), 1.0, 0.0)
            hots[:, part] = same.astype(BF)
            count[...] += same
            return carry

        lax.fori_loop(0, hots.shape[1] // 128, step, 0)
        total = jnp.sum(count[...], axis=1, keepdims=True)
        count[...] = jnp.broadcast_to(jnp.maximum(total, 1.0), count.shape)

    def edge_weights(table, at, w_edge):
        table[at : at + 128, :] = jnp.zeros((128, width), BF)
        table[at : at + 4, :] = w_edge

    def mean(hots, messages, count):
        return dot(hots, messages) / jnp.concatenate([count] * (width // 128), axis=1)

    edge_rows(enc_rows, enc_feat, enc_sender, n_grid, SLOTS_GRID)
    sender_hot(enc_rows, enc_hot, n_grid, N_DOM * SLOTS_GRID)
    edge_weights(enc_table, n_grid, w_enc_edge[...])

    def enc_local(i, carry):
        part = pl.ds(pl.multiple_of(i * 512, 512), 512)
        enc_sum[part, :] = dot(enc_hot[part, 0 : n_grid + 128], enc_table[...])
        return carry

    lax.fori_loop(0, enc_sum.shape[0] // 512, enc_local, 0)
    receiver_hot(enc_offset, enc_to, enc_count)

    wait_for(grid_got, 16, recv_sem.at[0])

    def embed_lent(i, carry):
        part = pl.ds(pl.multiple_of(i * 256, 256), 256)
        latent = silu(dot(grid_got[part, 0:channels], w_embed_held[...])).astype(BF)
        enc_lent[part, :] = dot(latent, w_grid_send_held[...]).astype(BF)
        return carry

    lax.fori_loop(0, enc_lent.shape[0] // 256, embed_lent, 0)

    def enc_remote(i, carry):
        part = pl.ds(pl.multiple_of(i * 512, 512), 512)
        total = enc_sum[part, :] + dot(enc_hot[part, n_grid + 128 :], enc_lent[...])
        enc_msg[part, :] = silu(total).astype(BF)
        return carry

    lax.fori_loop(0, enc_sum.shape[0] // 512, enc_remote, 0)
    mesh_now[...] = mean(enc_to[...], enc_msg[...], enc_count[...]).astype(BF)

    def lend(k, lent, values):
        picks = jnp.concatenate([hot(lent[...], 0.0), hot(lent[...], 128.0)], axis=1)
        stacked = jnp.concatenate([values[:, 0:half], values[:, half:]], axis=0)
        mesh_out[k] = dot(picks, stacked).astype(BF)
        send_blocks(
            lambda r: mesh_out.at[k, pl.ds(pl.multiple_of(r * 16, 16), 16)],
            mesh_got.at[k],
            16,
            send_sem.at[k + 1],
            recv_sem.at[k + 1],
        )

    def borrow(k):
        wait_for(mesh_got.at[k], 16, recv_sem.at[k + 1])
        got = mesh_got[k].astype(F32).reshape(N_DOM, 16, half)
        low = got[:, 0:8, :].reshape(N_DOM * 8, half)
        high = got[:, 8:16, :].reshape(N_DOM * 8, half)
        mesh_table[256:512, :] = jnp.concatenate([low, high], axis=1).astype(BF)

    def messages_of(hots, messages):
        def step(i, carry):
            part = pl.ds(pl.multiple_of(i * 512, 512), 512)
            messages[part, :] = silu(dot(hots[part, :], mesh_table[...])).astype(BF)
            return carry

        lax.fori_loop(0, hots.shape[0] // 512, step, 0)

    for load in loads[3:]:
        load.wait()
    for k in range(2):
        values = dot(mesh_now[...], w_proc_send_held[k]).astype(BF)
        lend(k, lend_mesh, values)
        mesh_table[0:128, :] = values
        edge_weights(mesh_table, 128, w_proc_edge[k])
        if k == 0:
            edge_rows(mesh_rows, mesh_feat, mesh_sender, n_mesh, SLOTS_MESH)
            sender_hot(mesh_rows, mesh_hot, n_mesh, N_DOM * SLOTS_MESH)
            receiver_hot(mesh_offset, mesh_to, mesh_count)
        else:
            edge_rows(dec_rows, dec_feat, dec_sender, n_mesh, SLOTS_MESH)
            sender_hot(dec_rows, dec_hot, n_mesh, N_DOM * SLOTS_MESH)
        borrow(k)
        messages_of(mesh_hot, mesh_msg)
        mesh_mean = mean(mesh_to[...], mesh_msg[...], mesh_count[...]).astype(BF)
        update = silu(dot(mesh_mean, w_proc_node_held[k]))
        mesh_now[...] = (mesh_now[...].astype(F32) + update).astype(BF)

    lend(2, lend_dec, mesh_now[...])
    mesh_table[0:128, :] = mesh_now[...]
    edge_weights(mesh_table, 128, w_dec_edge[...])
    receiver_hot(dec_offset, dec_to, dec_count, dec_block)
    borrow(2)
    messages_of(dec_hot, dec_msg)

    def decode(i, carry):
        part = pl.ds(pl.multiple_of(i * 256, 256), 256)
        grid_mean = mean(dec_to[part, :], dec_msg[...], dec_count[part, :]).astype(BF)
        mixed = dot(grid_mean, w_dec_held[...]) + dot(grid_latent[part, :], w_skip_held[...])
        out[:, part] = dot_turned(w_out_held[...], silu(mixed).astype(BF)).astype(BF)
        return carry

    lax.fori_loop(0, n_grid // 256, decode, 0)

    wait_for(lists_got, 1, lists_sem.at[0])
    wait_for(grid_out, 16, send_sem.at[0])
    for k in range(3):
        wait_for(mesh_out.at[k], 16, send_sem.at[k + 1])


def local(
    grid_in,
    w_embed,
    w_grid_send,
    enc_feat,
    w_enc_edge,
    enc_sender,
    enc_offset,
    grid_rows,
    w_proc_send,
    w_proc_edge,
    w_proc_node,
    mesh_feat,
    mesh_sender,
    mesh_offset,
    mesh_rows,
    w_skip,
    w_dec,
    w_dec_edge,
    dec_feat,
    dec_sender,
    dec_offset,
    dec_block,
    dec_rows,
    w_out,
):
    n_grid = grid_in.shape[0]
    width = w_embed.shape[1]
    n_mesh = 128
    enc, mesh, dec = enc_sender.shape[0], mesh_sender.shape[0], dec_sender.shape[0]
    operands = (
        grid_in.T,
        w_embed,
        w_grid_send,
        enc_feat,
        w_enc_edge,
        enc_sender.reshape(1, enc),
        enc_offset.reshape(1, enc),
        grid_rows.T,
        mesh_rows.T,
        dec_rows.T,
        w_proc_send,
        w_proc_edge,
        w_proc_node,
        mesh_feat,
        mesh_sender.reshape(1, mesh),
        mesh_offset.reshape(1, mesh),
        w_skip,
        w_dec,
        w_dec_edge,
        dec_feat,
        dec_sender.reshape(1, dec),
        dec_offset.reshape(1, dec),
        dec_block.reshape(1, dec_block.shape[0]),
        w_out.T,
    )
    whole = pl.BlockSpec(memory_space=pltpu.VMEM)
    far = pl.BlockSpec(memory_space=pl.ANY)
    in_specs = [whole] * len(operands)
    for i in (0, 1, 2, 10, 12, 16, 17, 23):
        in_specs[i] = far
    in_specs[22] = pl.BlockSpec(memory_space=pltpu.SMEM)
    forecast = pl.pallas_call(
        kernel,
        out_shape=jax.ShapeDtypeStruct((w_out.shape[1], n_grid), BF),
        in_specs=in_specs,
        out_specs=whole,
        scratch_shapes=[
            pltpu.VMEM((N_DOM, 1, 128), jnp.int32),
            pltpu.VMEM((N_DOM, 1, 128), jnp.int32),
            pltpu.VMEM((512, 256), BF),
            pltpu.VMEM((512, 256), BF),
            pltpu.VMEM((3, 512, 256), BF),
            pltpu.VMEM((3, 512, 256), BF),
            pltpu.VMEM((512, 128), F32),
            pltpu.VMEM((512, 128), F32),
            pltpu.VMEM((512, 128), F32),
            pltpu.VMEM((8, enc), F32),
            pltpu.VMEM((8, mesh), F32),
            pltpu.VMEM((8, dec), F32),
            pltpu.VMEM((enc, n_grid + 128 + 512), BF),
            pltpu.VMEM((mesh, 512), BF),
            pltpu.VMEM((dec, 512), BF),
            pltpu.VMEM((n_mesh, enc), BF),
            pltpu.VMEM((n_mesh, mesh), BF),
            pltpu.VMEM((n_grid, dec), BF),
            pltpu.VMEM((n_mesh, 128), F32),
            pltpu.VMEM((n_mesh, 128), F32),
            pltpu.VMEM((n_grid, 128), F32),
            pltpu.VMEM((n_grid, width), BF),
            pltpu.VMEM((n_grid + 128, width), BF),
            pltpu.VMEM((512, width), BF),
            pltpu.VMEM((512, width), BF),
            pltpu.VMEM((enc, width), F32),
            pltpu.VMEM((enc, width), BF),
            pltpu.VMEM((mesh, width), BF),
            pltpu.VMEM((dec, width), BF),
            pltpu.VMEM((n_mesh, width), BF),
            pltpu.VMEM((256, grid_in.shape[1]), BF),
            pltpu.VMEM(grid_in.shape[::-1], BF),
            pltpu.VMEM(w_embed.shape, BF),
            pltpu.VMEM(w_grid_send.shape, BF),
            pltpu.VMEM(w_proc_send.shape, BF),
            pltpu.VMEM(w_proc_node.shape, BF),
            pltpu.VMEM(w_skip.shape, BF),
            pltpu.VMEM(w_dec.shape, BF),
            pltpu.VMEM(w_out.shape[::-1], BF),
            pltpu.SemaphoreType.DMA((8,)),
            pltpu.SemaphoreType.DMA((2,)),
            pltpu.SemaphoreType.DMA((4,)),
            pltpu.SemaphoreType.DMA((4,)),
        ],
        compiler_params=pltpu.CompilerParams(
            collective_id=0, has_side_effects=True, vmem_limit_bytes=56 * 1024 * 1024
        ),
        name="graph_weather",
    )(*operands)
    return forecast.T


def solution(mesh):
    in_specs = (
        P(("member", "dom"), None),
        P(),
        P(),
        P(None, "dom"),
        P(),
        P("dom"),
        P("dom"),
        P("dom", None),
        P(),
        P(),
        P(),
        P(None, "dom"),
        P("dom"),
        P("dom"),
        P("dom", None),
        P(),
        P(),
        P(),
        P(None, "dom"),
        P("dom"),
        P("dom"),
        P("dom"),
        P("dom", None),
        P(),
    )
    out_specs = P(("member", "dom"), None)
    return jax.shard_map(local, mesh=mesh, in_specs=in_specs, out_specs=out_specs, check_vma=False)
```

```python
import jax
import jax.numpy as jnp
from jax import lax
from jax.experimental import pallas as pl
from jax.experimental.pallas import tpu as pltpu
from jax.sharding import PartitionSpec as P

N_Z, N_X = 8, 4
N_DOM = N_Z * N_X
SLOTS_GRID = 16
SLOTS_MESH = 8
BF = jnp.bfloat16
F32 = jnp.float32


def silu_of_half(half):
    return half + half * jnp.tanh(half)


def silu(v):
    return silu_of_half(0.5 * v)


def dot(a, b):
    return jnp.dot(a, b, preferred_element_type=F32)


def dot_turned(a, b):
    return lax.dot_general(a, b, (((1,), (1,)), ((), ())), preferred_element_type=F32)


def lanes(shape):
    return lax.broadcasted_iota(jnp.int32, shape, 1).astype(F32)


def rows(shape):
    return lax.broadcasted_iota(jnp.int32, shape, 0).astype(F32)


def hot(index, offset, value=1.0):
    return jnp.where(index == lanes(index.shape) + offset, value, 0.0).astype(BF)


def hops(offset):
    dz, dx = offset
    return min(dz, N_Z - dz) + min(dx, N_X - dx)


OFFSETS = [(dz, dx) for dz in range(N_Z) for dx in range(N_X) if (dz, dx) != (0, 0)]
FAR_FIRST = sorted(OFFSETS, key=lambda offset: -hops(offset))


def plain_slot(dz, dx):
    return (dz % N_Z) * N_X + dx % N_X


def far_slot(dz, dx):
    dz = dz % N_Z
    return (dz + 4 if dz < 3 else dz - 3 if dz < 7 else 7) * N_X + dx % N_X


def kernel(
    grid_in,
    w_embed,
    w_grid_send,
    enc_feat,
    w_enc_edge,
    enc_sender,
    enc_offset,
    grid_list,
    mesh_list,
    dec_list,
    w_proc_send,
    w_proc_edge,
    w_proc_node,
    mesh_feat,
    mesh_sender,
    mesh_offset,
    w_skip,
    w_dec,
    w_dec_edge,
    dec_feat,
    dec_sender,
    dec_offset,
    dec_block,
    w_out,
    out,
    lists_out,
    lists_got,
    grid_out,
    grid_got,
    mesh_out,
    mesh_got,
    lend_grid,
    lend_mesh,
    lend_dec,
    lend_hot,
    enc_rows,
    mesh_rows,
    dec_rows,
    enc_hot,
    mesh_hot,
    dec_hot,
    enc_to,
    mesh_to,
    dec_to,
    enc_count,
    mesh_count,
    dec_count,
    grid_latent,
    enc_table,
    enc_lent,
    mesh_table,
    edge_sum,
    edge_msg,
    mesh_now,
    mesh_mean,
    mixed,
    grid_turned,
    grid_held,
    w_embed_held,
    w_grid_send_held,
    w_proc_send_held,
    w_proc_node_held,
    w_skip_held,
    w_dec_held,
    w_out_held,
    load_sem,
    lists_sem,
    send_sem,
    recv_sem,
):
    me = lax.axis_index("dom")
    me_z, me_x = me // N_X, lax.rem(me, N_X)
    width = w_embed.shape[1]
    half = width // 2
    quarter = width // 4
    channels, n_grid = grid_in.shape
    n_mesh = mesh_to.shape[0]
    near = n_grid + 128

    def peer(dz, dx):
        return lax.rem(me_z + dz, N_Z) * N_X + lax.rem(me_x + dx, N_X)

    def send(source, target, out_sem, in_sem, offset):
        pltpu.make_async_remote_copy(
            src_ref=source,
            dst_ref=target,
            send_sem=out_sem,
            recv_sem=in_sem,
            device_id={"dom": peer(*offset)},
            device_id_type=pl.DeviceIdType.MESH,
        ).start()

    def wait_for(part, sem):
        pltpu.make_async_copy(part, part, sem).wait()

    barrier = pltpu.get_barrier_semaphore()
    for offset in FAR_FIRST:
        pl.semaphore_signal(
            barrier,
            inc=1,
            device_id={"dom": peer(*offset)},
            device_id_type=pl.DeviceIdType.MESH,
        )

    loads = [
        pltpu.make_async_copy(held_from, held, load_sem.at[i])
        for i, (held_from, held) in enumerate(
            (
                (grid_in, grid_held),
                (w_embed, w_embed_held),
                (w_grid_send, w_grid_send_held),
                (w_proc_send, w_proc_send_held),
                (w_proc_node, w_proc_node_held),
                (w_skip, w_skip_held),
                (w_dec, w_dec_held),
                (w_out, w_out_held),
            )
        )
    ]
    for load in loads:
        load.start()

    slots = jnp.concatenate([grid_list[...], mesh_list[...], dec_list[...]], axis=0).astype(F32)
    slots = jnp.concatenate([slots, jnp.zeros((N_DOM, 96), F32)], axis=1)
    slots = jnp.transpose(jnp.concatenate([slots, jnp.zeros((96, 128), F32)], axis=0))
    for p in range(N_DOM):
        lists_out[p] = slots[p : p + 1, :].astype(jnp.int32)

    lists_got[0:1] = jnp.zeros((1, 1, 128), jnp.int32)
    own = 16 * far_slot(0, 0)
    grid_got[own : own + 16, :] = jnp.zeros((16, 256), BF)
    for k in range(3):
        for h in range(2):
            mesh_got[k, h, 0:16, :] = jnp.zeros((16, quarter), BF)

    for load in loads[0:3]:
        load.wait()

    def embed(i, carry):
        part = pl.ds(pl.multiple_of(i * 256, 256), 256)
        grid_turned[...] = jnp.transpose(grid_held[:, part])
        latent = silu(dot(grid_turned[...], w_embed_held[...])).astype(BF)
        grid_latent[part, :] = latent
        enc_table[part, :] = dot(latent, w_grid_send_held[...]).astype(BF)
        return carry

    lax.fori_loop(0, n_grid // 256, embed, 0)

    pl.semaphore_wait(barrier, N_DOM - 1)
    for dz, dx in FAR_FIRST:
        send(
            lists_out.at[pl.ds(peer(dz, dx), 1)],
            lists_got.at[pl.ds(plain_slot(-dz, -dx), 1)],
            lists_sem.at[0],
            lists_sem.at[1],
            (dz, dx),
        )

    def edge_rows(scratch, feat, sender, n_local, n_slots, first):
        value = sender[...]
        shifted = jnp.maximum(value - n_local, 0)
        log_slots = n_slots.bit_length() - 1
        giver = shifted >> log_slots
        dz = ((giver >> 2) - me_z) & (N_Z - 1)
        dx = ((giver & (N_X - 1)) - me_x) & (N_X - 1)
        if first:
            dz = jnp.where(dz < 3, dz + 4, jnp.where(dz < 7, dz - 3, 7))
        lent = ((dz * N_X + dx) << log_slots) + (shifted & (n_slots - 1))
        local = value < n_local
        scratch[...] = jnp.zeros_like(scratch)
        scratch[0:4, :] = 0.5 * feat[...].astype(F32)
        scratch[4:5, :] = jnp.where(local, value, -1).astype(F32)
        scratch[5:6, :] = jnp.where(local, -1, lent).astype(F32)

    def sender_hot(scratch, hots, n_local, n_lent):
        def step(i, carry):
            part = pl.ds(pl.multiple_of(i * 128, 128), 128)
            turned = jnp.transpose(
                jnp.concatenate([scratch[:, part], jnp.zeros((120, 128), F32)], axis=0)
            )
            local = jnp.broadcast_to(turned[:, 4:5], (128, 128))
            lent = jnp.broadcast_to(turned[:, 5:6], (128, 128))
            for j in range(n_local // 128):
                hots[part, 128 * j : 128 * j + 128] = hot(local, 128.0 * j, 0.5)
            hots[part, n_local : n_local + 128] = turned.astype(BF)
            for j in range(n_lent // 128):
                at = n_local + 128 + 128 * j
                hots[part, at : at + 128] = hot(lent, 128.0 * j, 0.5)
            return carry

        lax.fori_loop(0, hots.shape[0] // 128, step, 0, unroll=4)

    def receiver_hot(target, hots, count, block=None):
        n_rows = hots.shape[0]
        count[...] = jnp.zeros_like(count)

        def step(i, carry):
            part = pl.ds(pl.multiple_of(i * 128, 128), 128)
            wanted = target[:, part]
            if block is not None:
                wanted = jnp.where(wanted >= 0, wanted + 128 * block[0, i], -1)
            wanted = jnp.broadcast_to(wanted.astype(F32), (n_rows, 128))
            same = jnp.where(wanted == rows((n_rows, 128)), 1.0, 0.0)
            hots[:, part] = same.astype(BF)
            count[...] += same
            return carry

        lax.fori_loop(0, hots.shape[1] // 128, step, 0, unroll=2)
        total = jnp.sum(count[...], axis=1, keepdims=True)
        count[...] = jnp.broadcast_to(jnp.maximum(total, 1.0), count.shape)

    def edge_weights(table, at, w_edge):
        table[at : at + 128, :] = jnp.zeros((128, width), BF)
        table[at : at + 4, :] = w_edge

    def mean(hots, messages, count):
        columns = messages.shape[1]
        return dot(hots, messages) / jnp.concatenate([count] * (columns // 128), axis=1)

    edge_rows(enc_rows, enc_feat, enc_sender, n_grid, SLOTS_GRID, True)
    sender_hot(enc_rows, enc_hot, n_grid, N_DOM * SLOTS_GRID)
    receiver_hot(enc_offset, enc_to, enc_count)
    edge_weights(enc_table, n_grid, w_enc_edge[...])

    wait_for(lists_got.at[pl.ds(1, N_DOM - 1)], lists_sem.at[1])
    listed = lists_got[:, 0, :].astype(F32)
    listed = jnp.transpose(jnp.concatenate([listed, jnp.zeros((96, 128), F32)], axis=0))
    for q in range(N_DOM):
        lend_grid[16 * q : 16 * q + 16, :] = jnp.broadcast_to(listed[0:16, q : q + 1], (16, 128))
        for lent, first in ((lend_mesh, 16), (lend_dec, 24)):
            column = jnp.broadcast_to(listed[first : first + 8, q : q + 1], (8, 128))
            lent[16 * q : 16 * q + 8, :] = column
            lent[16 * q + 8 : 16 * q + 16, :] = column + 128.0

    for group, pair in ((0, (4, 5)), (0, (3, 2)), (1, (6, 7)), (1, (1, 0))):
        part = pl.ds(64 * min(pair), 128)
        picks = jnp.concatenate(
            [hot(lend_grid[part, :], 128.0 * j) for j in range(n_grid // 128)], axis=1
        )
        grid_out[part, channels - channels % 128 :] = jnp.zeros((128, 128), BF)
        grid_out[part, 0:channels] = dot_turned(picks, grid_held[...]).astype(BF)
        for dz in pair:
            for dx in (2, 1, 3, 0):
                if (dz, dx) != (0, 0):
                    send(
                        grid_out.at[pl.ds(16 * plain_slot(dz, dx), 16)],
                        grid_got.at[pl.ds(16 * far_slot(-dz, -dx), 16)],
                        send_sem.at[group],
                        recv_sem.at[group],
                        (dz, dx),
                    )

    def local_sums(hots, columns, table):
        def step(i, carry):
            part = pl.ds(pl.multiple_of(i * 512, 512), 512)
            edge_sum[part, :] = dot(hots[part, 0:columns], table)
            return carry

        lax.fori_loop(0, hots.shape[0] // 512, step, 0)

    local_sums(enc_hot, near, enc_table[...])
    edge_rows(mesh_rows, mesh_feat, mesh_sender, n_mesh, SLOTS_MESH, False)
    sender_hot(mesh_rows, mesh_hot, n_mesh, N_DOM * SLOTS_MESH)
    receiver_hot(mesh_offset, mesh_to, mesh_count)
    for k, lent in enumerate((lend_mesh, lend_dec)):
        lend_hot[k] = jnp.concatenate([hot(lent[...], 0.0), hot(lent[...], 128.0)], axis=1)

    def embed_lent(group):
        wait_for(
            grid_got.at[pl.ds(256 * group + 16 * group, 256 - 16 * group)], recv_sem.at[group]
        )
        part = pl.ds(256 * group, 256)
        latent = silu(dot(grid_got[part, 0:channels], w_embed_held[...])).astype(BF)
        enc_lent[...] = dot(latent, w_grid_send_held[...]).astype(BF)

    embed_lent(0)

    def enc_first(i, carry):
        part = pl.ds(pl.multiple_of(i * 512, 512), 512)
        edge_sum[part, :] += dot(enc_hot[part, near : near + 256], enc_lent[...])
        return carry

    lax.fori_loop(0, enc_hot.shape[0] // 512, enc_first, 0)
    embed_lent(1)

    def enc_second(i, carry):
        part = pl.ds(pl.multiple_of(i * 512, 512), 512)
        total = edge_sum[part, :] + dot(enc_hot[part, near + 256 :], enc_lent[...])
        edge_msg[part, :] = silu_of_half(total).astype(BF)
        return carry

    lax.fori_loop(0, enc_hot.shape[0] // 512, enc_second, 0)
    mesh_now[...] = mean(enc_to[...], edge_msg[0 : enc_to.shape[1], :], enc_count[...]).astype(BF)

    def lend(k, picks, values):
        for h in range(2):
            at = h * half
            stacked = jnp.concatenate(
                [values[:, at : at + quarter], values[:, at + quarter : at + half]], axis=0
            )
            mesh_out[k, h] = dot(picks, stacked).astype(BF)
            for dz, dx in FAR_FIRST:
                send(
                    mesh_out.at[k, h, pl.ds(16 * plain_slot(dz, dx), 16)],
                    mesh_got.at[k, h, pl.ds(16 * plain_slot(-dz, -dx), 16)],
                    send_sem.at[2 + 2 * k + h],
                    recv_sem.at[2 + 2 * k + h],
                    (dz, dx),
                )

    def borrow(k, h):
        wait_for(mesh_got.at[k, h, pl.ds(16, 16 * (N_DOM - 1))], recv_sem.at[2 + 2 * k + h])
        got = mesh_got[k, h].astype(F32).reshape(N_DOM, 16, quarter)
        low = got[:, 0:8, :].reshape(N_DOM * 8, quarter)
        high = got[:, 8:16, :].reshape(N_DOM * 8, quarter)
        return jnp.concatenate([low, high], axis=1).astype(BF)

    def messages_of(hots, table, h, unroll):
        at = h * half

        def step(i, carry):
            part = pl.ds(pl.multiple_of(i * 512, 512), 512)
            total = edge_sum[part, at : at + half] + dot(hots[part, 256:512], table)
            edge_msg[part, at : at + half] = silu_of_half(total).astype(BF)
            return carry

        lax.fori_loop(0, hots.shape[0] // 512, step, 0, unroll=unroll)

    for load in loads[3:]:
        load.wait()
    for k in range(2):
        values = dot(mesh_now[...], w_proc_send_held[k]).astype(BF)
        lend(k, lend_hot[0], values)
        mesh_table[0:128, :] = values
        edge_weights(mesh_table, 128, w_proc_edge[k])
        local_sums(mesh_hot, 256, mesh_table[...])
        if k == 0:
            edge_rows(dec_rows, dec_feat, dec_sender, n_mesh, SLOTS_MESH, False)
            sender_hot(dec_rows, dec_hot, n_mesh, N_DOM * SLOTS_MESH)
        else:
            receiver_hot(dec_offset, dec_to, dec_count, dec_block)

            def skip(i, carry):
                part = pl.ds(pl.multiple_of(i * 256, 256), 256)
                mixed[part, :] = dot(grid_latent[part, :], w_skip_held[...])
                return carry

            lax.fori_loop(0, n_grid // 256, skip, 0)
        for h in range(2):
            at = h * half
            messages_of(mesh_hot, borrow(k, h), h, 2)
            mesh_mean[:, at : at + half] = mean(
                mesh_to[...], edge_msg[0 : mesh_to.shape[1], at : at + half], mesh_count[...]
            ).astype(BF)
        update = silu(dot(mesh_mean[...], w_proc_node_held[k]))
        mesh_now[...] = (mesh_now[...].astype(F32) + update).astype(BF)

    lend(2, lend_hot[1], mesh_now[...])
    mesh_table[0:128, :] = mesh_now[...]
    edge_weights(mesh_table, 128, w_dec_edge[...])
    local_sums(dec_hot, 256, mesh_table[...])
    for h in range(2):
        at = h * half
        messages_of(dec_hot, borrow(2, h), h, 1)

        def decode(i, carry):
            part = pl.ds(pl.multiple_of(i * 256, 256), 256)
            grid_mean = mean(dec_to[part, :], edge_msg[:, at : at + half], dec_count[part, :])
            total = mixed[part, :] + dot(grid_mean.astype(BF), w_dec_held[at : at + half, :])
            if h == 0:
                mixed[part, :] = total
            else:
                out[:, part] = dot_turned(w_out_held[...], silu(total).astype(BF)).astype(BF)
            return carry

        lax.fori_loop(0, n_grid // 256, decode, 0)

    wait_for(lists_got.at[pl.ds(1, N_DOM - 1)], lists_sem.at[0])
    wait_for(grid_out.at[pl.ds(0, 256)], send_sem.at[0])
    wait_for(grid_out.at[pl.ds(272, 240)], send_sem.at[1])
    for k in range(3):
        for h in range(2):
            wait_for(mesh_out.at[k, h, pl.ds(16, 16 * (N_DOM - 1))], send_sem.at[2 + 2 * k + h])


def local(
    grid_in,
    w_embed,
    w_grid_send,
    enc_feat,
    w_enc_edge,
    enc_sender,
    enc_offset,
    grid_rows,
    w_proc_send,
    w_proc_edge,
    w_proc_node,
    mesh_feat,
    mesh_sender,
    mesh_offset,
    mesh_rows,
    w_skip,
    w_dec,
    w_dec_edge,
    dec_feat,
    dec_sender,
    dec_offset,
    dec_block,
    dec_rows,
    w_out,
):
    n_grid = grid_in.shape[0]
    width = w_embed.shape[1]
    n_mesh = 128
    enc, mesh, dec = enc_sender.shape[0], mesh_sender.shape[0], dec_sender.shape[0]
    operands = (
        grid_in.T,
        w_embed,
        w_grid_send,
        enc_feat,
        w_enc_edge,
        enc_sender.reshape(1, enc),
        enc_offset.reshape(1, enc),
        grid_rows.T,
        mesh_rows.T,
        dec_rows.T,
        w_proc_send,
        w_proc_edge,
        w_proc_node,
        mesh_feat,
        mesh_sender.reshape(1, mesh),
        mesh_offset.reshape(1, mesh),
        w_skip,
        w_dec,
        w_dec_edge,
        dec_feat,
        dec_sender.reshape(1, dec),
        dec_offset.reshape(1, dec),
        dec_block.reshape(1, dec_block.shape[0]),
        w_out.T,
    )
    whole = pl.BlockSpec(memory_space=pltpu.VMEM)
    far = pl.BlockSpec(memory_space=pl.ANY)
    in_specs = [whole] * len(operands)
    for i in (0, 1, 2, 10, 12, 16, 17, 23):
        in_specs[i] = far
    in_specs[22] = pl.BlockSpec(memory_space=pltpu.SMEM)
    forecast = pl.pallas_call(
        kernel,
        out_shape=jax.ShapeDtypeStruct((w_out.shape[1], n_grid), BF),
        in_specs=in_specs,
        out_specs=whole,
        scratch_shapes=[
            pltpu.VMEM((N_DOM, 1, 128), jnp.int32),
            pltpu.VMEM((N_DOM, 1, 128), jnp.int32),
            pltpu.VMEM((512, 256), BF),
            pltpu.VMEM((512, 256), BF),
            pltpu.VMEM((3, 2, 512, width // 4), BF),
            pltpu.VMEM((3, 2, 512, width // 4), BF),
            pltpu.VMEM((512, 128), F32),
            pltpu.VMEM((512, 128), F32),
            pltpu.VMEM((512, 128), F32),
            pltpu.VMEM((2, 512, 256), BF),
            pltpu.VMEM((8, enc), F32),
            pltpu.VMEM((8, mesh), F32),
            pltpu.VMEM((8, dec), F32),
            pltpu.VMEM((enc, n_grid + 128 + 512), BF),
            pltpu.VMEM((mesh, 512), BF),
            pltpu.VMEM((dec, 512), BF),
            pltpu.VMEM((n_mesh, enc), BF),
            pltpu.VMEM((n_mesh, mesh), BF),
            pltpu.VMEM((n_grid, dec), BF),
            pltpu.VMEM((n_mesh, 128), F32),
            pltpu.VMEM((n_mesh, 128), F32),
            pltpu.VMEM((n_grid, 128), F32),
            pltpu.VMEM((n_grid, width), BF),
            pltpu.VMEM((n_grid + 128, width), BF),
            pltpu.VMEM((256, width), BF),
            pltpu.VMEM((256, width), BF),
            pltpu.VMEM((max(enc, dec), width), F32),
            pltpu.VMEM((max(enc, dec), width), BF),
            pltpu.VMEM((n_mesh, width), BF),
            pltpu.VMEM((n_mesh, width), BF),
            pltpu.VMEM((n_grid, width), F32),
            pltpu.VMEM((256, grid_in.shape[1]), BF),
            pltpu.VMEM(grid_in.shape[::-1], BF),
            pltpu.VMEM(w_embed.shape, BF),
            pltpu.VMEM(w_grid_send.shape, BF),
            pltpu.VMEM(w_proc_send.shape, BF),
            pltpu.VMEM(w_proc_node.shape, BF),
            pltpu.VMEM(w_skip.shape, BF),
            pltpu.VMEM(w_dec.shape, BF),
            pltpu.VMEM(w_out.shape[::-1], BF),
            pltpu.SemaphoreType.DMA((8,)),
            pltpu.SemaphoreType.DMA((2,)),
            pltpu.SemaphoreType.DMA((8,)),
            pltpu.SemaphoreType.DMA((8,)),
        ],
        compiler_params=pltpu.CompilerParams(
            collective_id=0, has_side_effects=True, vmem_limit_bytes=56 * 1024 * 1024
        ),
        name="graph_weather",
    )(*operands)
    return forecast.T


def solution(mesh):
    in_specs = (
        P(("member", "dom"), None),
        P(),
        P(),
        P(None, "dom"),
        P(),
        P("dom"),
        P("dom"),
        P("dom", None),
        P(),
        P(),
        P(),
        P(None, "dom"),
        P("dom"),
        P("dom"),
        P("dom", None),
        P(),
        P(),
        P(),
        P(None, "dom"),
        P("dom"),
        P("dom"),
        P("dom"),
        P("dom", None),
        P(),
    )
    out_specs = P(("member", "dom"), None)
    return jax.shard_map(local, mesh=mesh, in_specs=in_specs, out_specs=out_specs, check_vma=False)
```

```python
import jax
import jax.numpy as jnp
from jax import lax
from jax.experimental import pallas as pl
from jax.experimental.pallas import tpu as pltpu
from jax.sharding import PartitionSpec as P

N_Z, N_X = 8, 4
N_DOM = N_Z * N_X
SLOTS_GRID = 16
SLOTS_MESH = 8
BF = jnp.bfloat16
F32 = jnp.float32
N_LOADS = 24


def silu_of_half(half):
    return half + half * jnp.tanh(half)


def silu(v):
    return silu_of_half(0.5 * v)


def dot(a, b):
    return jnp.dot(a, b, preferred_element_type=F32)


def dot_turned(a, b):
    return lax.dot_general(a, b, (((1,), (1,)), ((), ())), preferred_element_type=F32)


def lanes(shape):
    return lax.broadcasted_iota(jnp.int32, shape, 1).astype(F32)


def rows(shape):
    return lax.broadcasted_iota(jnp.int32, shape, 0).astype(F32)


def hot(index, offset, value=1.0):
    return jnp.where(index == lanes(index.shape) + offset, value, 0.0).astype(BF)


def hops(offset):
    dz, dx = offset
    return min(dz, N_Z - dz) + min(dx, N_X - dx)


OFFSETS = [(dz, dx) for dz in range(N_Z) for dx in range(N_X) if (dz, dx) != (0, 0)]
FAR_FIRST = sorted(OFFSETS, key=lambda offset: -hops(offset))


def slot(dz, dx):
    return (dz % N_Z) * N_X + dx % N_X


def kernel(*refs):
    far, out, held = refs[0:N_LOADS], refs[N_LOADS], refs[N_LOADS + 1 : 2 * N_LOADS + 1]
    (
        grid_list,
        mesh_list,
        dec_list,
        grid_in,
        w_embed,
        w_grid_send,
        enc_sender,
        enc_feat,
        w_enc_edge,
        enc_offset,
        mesh_sender,
        mesh_feat,
        w_proc_edge,
        mesh_offset,
        w_proc_send,
        w_proc_node,
        dec_sender,
        dec_feat,
        w_dec_edge,
        dec_offset,
        dec_block,
        w_skip,
        w_dec,
        w_out,
    ) = held
    (
        lists_out,
        lists_got,
        rows_out,
        rows_got,
        lend_grid,
        lend_mesh,
        lend_dec,
        lend_hot,
        enc_rows,
        mesh_rows,
        dec_rows,
        enc_hot,
        mesh_hot,
        dec_hot,
        enc_to,
        mesh_to,
        dec_to,
        enc_count,
        mesh_count,
        block_count,
        dec_count,
        running,
        grid_turned,
        grid_latent,
        enc_table,
        enc_lent,
        mesh_table,
        edge_sum,
        edge_msg,
        dec_msg,
        mesh_now,
        mesh_mean,
        grid_mean,
        mixed,
        rank,
        order,
        keep,
        last,
        load_sem,
        lists_sem,
        send_sem,
        recv_sem,
    ) = refs[2 * N_LOADS + 1 :]
    me = lax.axis_index("dom")
    me_z, me_x = me // N_X, lax.rem(me, N_X)
    width = w_embed.shape[1]
    half = width // 2
    quarter = width // 4
    channels, n_grid = grid_in.shape
    n_mesh = mesh_to.shape[0]
    n_edge_blocks = dec_block.shape[1]
    n_blocks = n_grid // 128
    near = n_grid + 128

    def peer(dz, dx):
        return lax.rem(me_z + dz, N_Z) * N_X + lax.rem(me_x + dx, N_X)

    def send(source, target, out_sem, in_sem, offset):
        pltpu.make_async_remote_copy(
            src_ref=source,
            dst_ref=target,
            send_sem=out_sem,
            recv_sem=in_sem,
            device_id={"dom": peer(*offset)},
            device_id_type=pl.DeviceIdType.MESH,
        ).start()

    def wait_for(part, sem):
        pltpu.make_async_copy(part, part, sem).wait()

    barrier = pltpu.get_barrier_semaphore()
    for offset in FAR_FIRST:
        pl.semaphore_signal(
            barrier,
            inc=1,
            device_id={"dom": peer(*offset)},
            device_id_type=pl.DeviceIdType.MESH,
        )

    loads = [
        pltpu.make_async_copy(source, target, load_sem.at[i])
        for i, (source, target) in enumerate(zip(far, held))
    ]
    for load in loads:
        load.start()

    lists_got[0:1] = jnp.zeros((1, 1, 128), jnp.int32)
    for x in range(4):
        for h in range(2):
            rows_got[x, h, 0:16, :] = jnp.zeros((16, quarter), BF)

    for load in loads[0:3]:
        load.wait()
    slots = jnp.concatenate([grid_list[...], mesh_list[...], dec_list[...]], axis=0).astype(F32)
    slots = jnp.concatenate([slots, jnp.zeros((N_DOM, 96), F32)], axis=1)
    slots = jnp.transpose(jnp.concatenate([slots, jnp.zeros((96, 128), F32)], axis=0))
    for p in range(N_DOM):
        lists_out[p] = slots[p : p + 1, :].astype(jnp.int32)

    pl.semaphore_wait(barrier, N_DOM - 1)
    for dz, dx in FAR_FIRST:
        send(
            lists_out.at[pl.ds(peer(dz, dx), 1)],
            lists_got.at[pl.ds(slot(-dz, -dx), 1)],
            lists_sem.at[0],
            lists_sem.at[1],
            (dz, dx),
        )

    for load in loads[3:6]:
        load.wait()
    grid_turned[:, channels - channels % 128 :] = jnp.zeros((n_grid, 128), BF)
    grid_turned[:, 0:channels] = jnp.transpose(grid_in[...])

    def embed(i, carry):
        part = pl.ds(pl.multiple_of(i * 512, 512), 512)
        latent = silu(dot(grid_turned[part, 0:channels], w_embed[...])).astype(BF)
        grid_latent[part, :] = latent
        enc_table[part, :] = dot(latent, w_grid_send[...]).astype(BF)
        return carry

    lax.fori_loop(0, n_grid // 512, embed, 0)

    def edge_rows(scratch, feat, sender, n_local, n_slots):
        value = sender[...]
        shifted = jnp.maximum(value - n_local, 0)
        giver = shifted >> (n_slots.bit_length() - 1)
        listed = shifted & (n_slots - 1)
        dz = ((giver >> 2) - me_z) & (N_Z - 1)
        dx = ((giver & (N_X - 1)) - me_x) & (N_X - 1)
        lent = ((listed >> 3) << 8) + ((dz * N_X + dx) << 3) + (listed & 7)
        local = value < n_local
        scratch[...] = jnp.zeros_like(scratch)
        scratch[0:4, :] = 0.5 * feat[...].astype(F32)
        scratch[4:5, :] = jnp.where(local, value, -1).astype(F32)
        scratch[5:6, :] = jnp.where(local, -1, lent).astype(F32)

    def sender_hot(scratch, hots, n_local, n_lent):
        def step(i, carry):
            part = pl.ds(pl.multiple_of(i * 128, 128), 128)
            turned = jnp.transpose(
                jnp.concatenate([scratch[:, part], jnp.zeros((120, 128), F32)], axis=0)
            )
            local = jnp.broadcast_to(turned[:, 4:5], (128, 128))
            lent = jnp.broadcast_to(turned[:, 5:6], (128, 128))
            for j in range(n_local // 128):
                hots[part, 128 * j : 128 * j + 128] = hot(local, 128.0 * j, 0.5)
            hots[part, n_local : n_local + 128] = turned.astype(BF)
            for j in range(n_lent // 128):
                at = n_local + 128 + 128 * j
                hots[part, at : at + 128] = hot(lent, 128.0 * j, 0.5)
            return carry

        lax.fori_loop(0, hots.shape[0] // 128, step, 0, unroll=8)

    def receiver_hot(target, hots, count):
        n_rows = hots.shape[0]
        count[...] = jnp.zeros_like(count)

        def step(i, carry):
            part = pl.ds(pl.multiple_of(i * 128, 128), 128)
            wanted = jnp.broadcast_to(target[:, part].astype(F32), (n_rows, 128))
            same = jnp.where(wanted == rows((n_rows, 128)), 1.0, 0.0)
            hots[:, part] = same.astype(BF)
            count[...] += same
            return carry

        lax.fori_loop(0, hots.shape[1] // 128, step, 0, unroll=4)
        total = jnp.sum(count[...], axis=1, keepdims=True)
        count[...] = jnp.broadcast_to(1.0 / jnp.maximum(total, 1.0), count.shape)

    def edge_weights(table, at, w_edge):
        table[at : at + 128, :] = jnp.zeros((128, width), BF)
        table[at : at + 4, :] = w_edge

    def mean(hots, messages, count):
        columns = messages.shape[1]
        return dot(hots, messages) * jnp.concatenate([count] * (columns // 128), axis=1)

    for load in loads[6:10]:
        load.wait()
    edge_rows(enc_rows, enc_feat, enc_sender, n_grid, SLOTS_GRID)
    sender_hot(enc_rows, enc_hot, n_grid, N_DOM * SLOTS_GRID)
    edge_weights(enc_table, n_grid, w_enc_edge[...])

    def ship(x, h):
        for dz, dx in FAR_FIRST:
            send(
                rows_out.at[x, h, pl.ds(16 * slot(dz, dx), 16)],
                rows_got.at[x, h, pl.ds(16 * slot(-dz, -dx), 16)],
                send_sem.at[2 * x + h],
                recv_sem.at[2 * x + h],
                (dz, dx),
            )

    def arrive(x, h):
        wait_for(rows_got.at[x, h, pl.ds(16, 16 * (N_DOM - 1))], recv_sem.at[2 * x + h])
        got = rows_got[x, h].astype(F32).reshape(N_DOM, 16, quarter)
        low = got[:, 0:8, :].reshape(N_DOM * 8, quarter)
        high = got[:, 8:16, :].reshape(N_DOM * 8, quarter)
        return jnp.concatenate([low, high], axis=1).astype(BF)

    wait_for(lists_got.at[pl.ds(1, N_DOM - 1)], lists_sem.at[1])
    listed = lists_got[:, 0, :].astype(F32)
    listed = jnp.transpose(jnp.concatenate([listed, jnp.zeros((96, 128), F32)], axis=0))
    for h in range(2):
        for q in range(N_DOM):
            lend_grid[h, 8 * q : 8 * q + 8, :] = jnp.broadcast_to(
                listed[8 * h : 8 * h + 8, q : q + 1], (8, 128)
            )
        picks = jnp.concatenate(
            [hot(lend_grid[h], 128.0 * j) for j in range(n_grid // 128)], axis=1
        )
        lent = dot(picks, grid_turned[...]).reshape(N_DOM, 8, 2 * quarter)
        lent = jnp.concatenate([lent[:, :, 0:quarter], lent[:, :, quarter:]], axis=1)
        rows_out[0, h] = lent.reshape(16 * N_DOM, quarter).astype(BF)
        ship(0, h)

    for q in range(N_DOM):
        for lent, first in ((lend_mesh, 16), (lend_dec, 24)):
            column = jnp.broadcast_to(listed[first : first + 8, q : q + 1], (8, 128))
            lent[16 * q : 16 * q + 8, :] = column
            lent[16 * q + 8 : 16 * q + 16, :] = column + 128.0
    for k, lent in enumerate((lend_mesh, lend_dec)):
        lend_hot[k] = jnp.concatenate([hot(lent[...], 0.0), hot(lent[...], 128.0)], axis=1)

    def local_sums(hots, columns, table):
        def step(i, carry):
            part = pl.ds(pl.multiple_of(i * 1024, 1024), 1024)
            edge_sum[part, :] = dot(hots[part, 0:columns], table)
            return carry

        lax.fori_loop(0, hots.shape[0] // 1024, step, 0)

    local_sums(enc_hot, near, enc_table[...])
    receiver_hot(enc_offset, enc_to, enc_count)

    def embed_lent(h):
        latent = silu(dot(arrive(0, h)[:, 0:channels], w_embed[...])).astype(BF)
        enc_lent[...] = dot(latent, w_grid_send[...]).astype(BF)

    embed_lent(0)

    def enc_first(i, carry):
        part = pl.ds(pl.multiple_of(i * 1024, 1024), 1024)
        edge_sum[part, :] += dot(enc_hot[part, near : near + 256], enc_lent[...])
        return carry

    lax.fori_loop(0, enc_hot.shape[0] // 1024, enc_first, 0)
    for load in loads[10:]:
        load.wait()
    embed_lent(1)

    def enc_second(i, carry):
        part = pl.ds(pl.multiple_of(i * 1024, 1024), 1024)
        total = edge_sum[part, :] + dot(enc_hot[part, near + 256 :], enc_lent[...])
        edge_msg[part, :] = silu_of_half(total).astype(BF)
        return carry

    lax.fori_loop(0, enc_hot.shape[0] // 1024, enc_second, 0)
    mesh_now[...] = mean(enc_to[...], edge_msg[0 : enc_to.shape[1], :], enc_count[...]).astype(BF)

    def lend(x, picks, values):
        for h in range(2):
            at = h * half
            stacked = jnp.concatenate(
                [values[:, at : at + quarter], values[:, at + quarter : at + half]], axis=0
            )
            rows_out[x, h] = dot(picks, stacked).astype(BF)
            ship(x, h)

    def messages_of(hots, table, h, by_block=False):
        at = h * half

        def step(i, carry):
            part = pl.ds(pl.multiple_of(i * 1024, 1024), 1024)
            total = edge_sum[part, at : at + half] + dot(hots[part, 256:512], table)
            message = silu_of_half(total).astype(BF)
            if by_block:
                blocks = pl.ds(pl.multiple_of(i * 8, 8), 8)
                dec_msg[blocks, :, at : at + half] = message.reshape(8, 128, half)
            else:
                edge_msg[part, at : at + half] = message
            return carry

        lax.fori_loop(0, hots.shape[0] // 1024, step, 0)

    def sort_blocks():
        def rank_of(b, carry):
            own = dec_block[0, b] * 32 + b
            below = jnp.int32(0)
            for other in range(n_edge_blocks):
                below += jnp.where(dec_block[0, other] * 32 + other < own, 1, 0)
            rank[b] = below
            return carry

        lax.fori_loop(0, n_edge_blocks, rank_of, 0)

        def block_at(t, carry):
            found = jnp.int32(0)
            for b in range(n_edge_blocks):
                found += jnp.where(rank[b] == t, b, 0)
            order[t] = found
            return carry

        lax.fori_loop(0, n_edge_blocks, block_at, 0)

        def kept(t, carry):
            same = dec_block[0, order[t]] == dec_block[0, order[jnp.maximum(t - 1, 0)]]
            keep[t] = jnp.where(same, 1, 0)
            return carry

        lax.fori_loop(0, n_edge_blocks, kept, 0)

        def last_of(g, carry):
            before, until = jnp.int32(0), jnp.int32(0)
            for b in range(n_edge_blocks):
                before += jnp.where(dec_block[0, b] < g, 1, 0)
                until += jnp.where(dec_block[0, b] <= g, 1, 0)
            last[g] = jnp.where(until > before, until, 0)
            return carry

        lax.fori_loop(0, n_blocks, last_of, 0)

    def dec_receivers():
        def step(b, carry):
            part = pl.ds(pl.multiple_of(b * 128, 128), 128)
            wanted = jnp.broadcast_to(dec_offset[:, part].astype(F32), (128, 128))
            same = jnp.where(wanted == rows((128, 128)), 1.0, 0.0)
            dec_to[b] = same.astype(BF)
            block_count[b] = jnp.broadcast_to(
                jnp.sum(same, axis=1, keepdims=True), (128, 128)
            )
            return carry

        lax.fori_loop(0, n_edge_blocks, step, 0, unroll=4)
        total = jnp.zeros((128, 128), F32)
        running[0] = jnp.zeros((128, width), F32)
        for t in range(n_edge_blocks):
            total = block_count[order[t]] + keep[t].astype(F32) * total
            running[t + 1, :, 0:128] = total
        for g in range(n_blocks):
            count = running[last[g], :, 0:128]
            dec_count[128 * g : 128 * g + 128, :] = 1.0 / jnp.maximum(count, 1.0)

    for k in range(2):
        values = dot(mesh_now[...], w_proc_send[k]).astype(BF)
        lend(1 + k, lend_hot[0], values)
        mesh_table[0:128, :] = values
        edge_weights(mesh_table, 128, w_proc_edge[k])
        if k == 0:
            edge_rows(mesh_rows, mesh_feat, mesh_sender, n_mesh, SLOTS_MESH)
            sender_hot(mesh_rows, mesh_hot, n_mesh, N_DOM * SLOTS_MESH)
            receiver_hot(mesh_offset, mesh_to, mesh_count)
            sort_blocks()
        local_sums(mesh_hot, 256, mesh_table[...])
        if k == 1:
            edge_rows(dec_rows, dec_feat, dec_sender, n_mesh, SLOTS_MESH)
            sender_hot(dec_rows, dec_hot, n_mesh, N_DOM * SLOTS_MESH)
            dec_receivers()
        for h in range(2):
            at = h * half
            messages_of(mesh_hot, arrive(1 + k, h), h)
            mesh_mean[:, at : at + half] = mean(
                mesh_to[...], edge_msg[0 : mesh_to.shape[1], at : at + half], mesh_count[...]
            ).astype(BF)
        update = silu(dot(mesh_mean[...], w_proc_node[k]))
        mesh_now[...] = (mesh_now[...].astype(F32) + update).astype(BF)

    lend(3, lend_hot[1], mesh_now[...])
    mesh_table[0:128, :] = mesh_now[...]
    edge_weights(mesh_table, 128, w_dec_edge[...])
    local_sums(dec_hot, 256, mesh_table[...])
    mixed[...] = dot(grid_latent[...], w_skip[...])
    for h in range(2):
        at = h * half
        messages_of(dec_hot, arrive(3, h), h, True)
        total = jnp.zeros((128, half), F32)
        for t in range(n_edge_blocks):
            block = dot(dec_to[order[t]], dec_msg[order[t], :, at : at + half])
            total = block + keep[t].astype(F32) * total
            running[t + 1, :, at : at + half] = total
        for g in range(n_blocks):
            count = dec_count[128 * g : 128 * g + 128, :]
            grid_mean[128 * g : 128 * g + 128, :] = (
                running[last[g], :, at : at + half] * jnp.concatenate([count] * (half // 128), axis=1)
            ).astype(BF)
        total = mixed[...] + dot(grid_mean[...], w_dec[at : at + half, :])
        if h == 0:
            mixed[...] = total
        else:
            out[...] = dot_turned(w_out[...], silu(total).astype(BF)).astype(BF)

    wait_for(lists_got.at[pl.ds(1, N_DOM - 1)], lists_sem.at[0])
    for x in range(4):
        for h in range(2):
            wait_for(rows_out.at[x, h, pl.ds(16, 16 * (N_DOM - 1))], send_sem.at[2 * x + h])


def local(
    grid_in,
    w_embed,
    w_grid_send,
    enc_feat,
    w_enc_edge,
    enc_sender,
    enc_offset,
    grid_rows,
    w_proc_send,
    w_proc_edge,
    w_proc_node,
    mesh_feat,
    mesh_sender,
    mesh_offset,
    mesh_rows,
    w_skip,
    w_dec,
    w_dec_edge,
    dec_feat,
    dec_sender,
    dec_offset,
    dec_block,
    dec_rows,
    w_out,
):
    n_grid = grid_in.shape[0]
    width = w_embed.shape[1]
    n_mesh = 128
    enc, mesh, dec = enc_sender.shape[0], mesh_sender.shape[0], dec_sender.shape[0]
    operands = (
        grid_rows.T,
        mesh_rows.T,
        dec_rows.T,
        grid_in.T,
        w_embed,
        w_grid_send,
        enc_sender.reshape(1, enc),
        enc_feat,
        w_enc_edge,
        enc_offset.reshape(1, enc),
        mesh_sender.reshape(1, mesh),
        mesh_feat,
        w_proc_edge,
        mesh_offset.reshape(1, mesh),
        w_proc_send,
        w_proc_node,
        dec_sender.reshape(1, dec),
        dec_feat,
        w_dec_edge,
        dec_offset.reshape(1, dec),
        dec_block.reshape(1, dec_block.shape[0]),
        w_skip,
        w_dec,
        w_out.T,
    )
    held = [
        pltpu.SMEM(operand.shape, operand.dtype)
        if i == 20
        else pltpu.VMEM(operand.shape, operand.dtype)
        for i, operand in enumerate(operands)
    ]
    most = max(enc, dec)
    forecast = pl.pallas_call(
        kernel,
        out_shape=pltpu.VMEM((w_out.shape[1], n_grid), BF),
        in_specs=[pl.BlockSpec(memory_space=pl.ANY)] * len(operands),
        out_specs=pl.BlockSpec(memory_space=pltpu.VMEM),
        scratch_shapes=held
        + [
            pltpu.VMEM((N_DOM, 1, 128), jnp.int32),
            pltpu.VMEM((N_DOM, 1, 128), jnp.int32),
            pltpu.VMEM((4, 2, 512, width // 4), BF),
            pltpu.VMEM((4, 2, 512, width // 4), BF),
            pltpu.VMEM((2, 256, 128), F32),
            pltpu.VMEM((512, 128), F32),
            pltpu.VMEM((512, 128), F32),
            pltpu.VMEM((2, 512, 256), BF),
            pltpu.VMEM((8, enc), F32),
            pltpu.VMEM((8, mesh), F32),
            pltpu.VMEM((8, dec), F32),
            pltpu.VMEM((enc, n_grid + 128 + 512), BF),
            pltpu.VMEM((mesh, 512), BF),
            pltpu.VMEM((dec, 512), BF),
            pltpu.VMEM((n_mesh, enc), BF),
            pltpu.VMEM((n_mesh, mesh), BF),
            pltpu.VMEM((dec // 128, 128, 128), BF),
            pltpu.VMEM((n_mesh, 128), F32),
            pltpu.VMEM((n_mesh, 128), F32),
            pltpu.VMEM((dec // 128, 128, 128), F32),
            pltpu.VMEM((n_grid, 128), F32),
            pltpu.VMEM((dec // 128 + 1, 128, width), F32),
            pltpu.VMEM((n_grid, 256), BF),
            pltpu.VMEM((n_grid, width), BF),
            pltpu.VMEM((n_grid + 128, width), BF),
            pltpu.VMEM((256, width), BF),
            pltpu.VMEM((256, width), BF),
            pltpu.VMEM((most, width), F32),
            pltpu.VMEM((max(enc, mesh), width), BF),
            pltpu.VMEM((dec // 128, 128, width), BF),
            pltpu.VMEM((n_mesh, width), BF),
            pltpu.VMEM((n_mesh, width), BF),
            pltpu.VMEM((n_grid, width // 2), BF),
            pltpu.VMEM((n_grid, width), F32),
            pltpu.SMEM((dec // 128,), jnp.int32),
            pltpu.SMEM((dec // 128,), jnp.int32),
            pltpu.SMEM((dec // 128,), jnp.int32),
            pltpu.SMEM((n_grid // 128,), jnp.int32),
            pltpu.SemaphoreType.DMA((N_LOADS,)),
            pltpu.SemaphoreType.DMA((2,)),
            pltpu.SemaphoreType.DMA((8,)),
            pltpu.SemaphoreType.DMA((8,)),
        ],
        compiler_params=pltpu.CompilerParams(
            collective_id=0, has_side_effects=True, vmem_limit_bytes=56 * 1024 * 1024
        ),
        name="graph_weather",
    )(*operands)
    return forecast.T


def solution(mesh):
    in_specs = (
        P(("member", "dom"), None),
        P(),
        P(),
        P(None, "dom"),
        P(),
        P("dom"),
        P("dom"),
        P("dom", None),
        P(),
        P(),
        P(),
        P(None, "dom"),
        P("dom"),
        P("dom"),
        P("dom", None),
        P(),
        P(),
        P(),
        P(None, "dom"),
        P("dom"),
        P("dom"),
        P("dom"),
        P("dom", None),
        P(),
    )
    out_specs = P(("member", "dom"), None)
    return jax.shard_map(local, mesh=mesh, in_specs=in_specs, out_specs=out_specs, check_vma=False)
```

```python
import jax
import jax.numpy as jnp
from jax import lax
from jax.experimental import pallas as pl
from jax.experimental.pallas import tpu as pltpu
from jax.sharding import PartitionSpec as P

N_Z, N_X = 8, 4
N_DOM = N_Z * N_X
SLOTS_GRID = 16
SLOTS_MESH = 8
BF = jnp.bfloat16
F32 = jnp.float32
N_LOADS = 24


def silu_of_half(half):
    return half + half * jnp.tanh(half)


def silu(v):
    return silu_of_half(0.5 * v)


def dot(a, b):
    return jnp.dot(a, b, preferred_element_type=F32)


def dot_turned(a, b):
    return lax.dot_general(a, b, (((1,), (1,)), ((), ())), preferred_element_type=F32)


def lanes(shape):
    return lax.broadcasted_iota(jnp.int32, shape, 1).astype(F32)


def rows(shape):
    return lax.broadcasted_iota(jnp.int32, shape, 0).astype(F32)


def hot(index, offset, value=1.0):
    return jnp.where(index == lanes(index.shape) + offset, value, 0.0).astype(BF)


def hops(offset):
    dz, dx = offset
    return min(dz, N_Z - dz) + min(dx, N_X - dx)


OFFSETS = [(dz, dx) for dz in range(N_Z) for dx in range(N_X) if (dz, dx) != (0, 0)]
FAR_FIRST = sorted(OFFSETS, key=lambda offset: -hops(offset))


def slot(dz, dx):
    return (dz % N_Z) * N_X + dx % N_X


def kernel(*refs):
    far, out, held = refs[0:N_LOADS], refs[N_LOADS], refs[N_LOADS + 1 : 2 * N_LOADS + 1]
    (
        grid_list,
        mesh_list,
        dec_list,
        grid_in,
        w_embed,
        w_grid_send,
        enc_sender,
        enc_feat,
        w_enc_edge,
        enc_offset,
        mesh_sender,
        mesh_feat,
        w_proc_edge,
        mesh_offset,
        w_proc_send,
        w_proc_node,
        dec_sender,
        dec_feat,
        w_dec_edge,
        dec_offset,
        dec_block,
        w_skip,
        w_dec,
        w_out,
    ) = held
    (
        lists_out,
        lists_got,
        rows_out,
        rows_got,
        wide_out,
        wide_got,
        lend_grid,
        lend_mesh,
        lend_dec,
        lend_hot,
        enc_rows,
        mesh_rows,
        dec_rows,
        enc_hot,
        mesh_hot,
        dec_hot,
        enc_to,
        mesh_to,
        dec_to,
        enc_count,
        mesh_count,
        block_count,
        dec_count,
        running,
        grid_turned,
        grid_latent,
        enc_table,
        enc_lent,
        mesh_table,
        edge_sum,
        dec_msg,
        mesh_now,
        grid_mean,
        mixed,
        rank,
        order,
        keep,
        last,
        load_sem,
        lists_sem,
        send_sem,
        recv_sem,
    ) = refs[2 * N_LOADS + 1 :]
    me = lax.axis_index("dom")
    me_z, me_x = me // N_X, lax.rem(me, N_X)
    width = w_embed.shape[1]
    half = width // 2
    quarter = width // 4
    channels, n_grid = grid_in.shape
    n_mesh = mesh_to.shape[0]
    n_edge_blocks = dec_block.shape[1]
    n_blocks = n_grid // 128
    near = n_grid + 128

    def peer(dz, dx):
        return lax.rem(me_z + dz, N_Z) * N_X + lax.rem(me_x + dx, N_X)

    def send(source, target, out_sem, in_sem, offset):
        pltpu.make_async_remote_copy(
            src_ref=source,
            dst_ref=target,
            send_sem=out_sem,
            recv_sem=in_sem,
            device_id={"dom": peer(*offset)},
            device_id_type=pl.DeviceIdType.MESH,
        ).start()

    def wait_for(part, sem):
        pltpu.make_async_copy(part, part, sem).wait()

    barrier = pltpu.get_barrier_semaphore()
    for offset in FAR_FIRST:
        pl.semaphore_signal(
            barrier,
            inc=1,
            device_id={"dom": peer(*offset)},
            device_id_type=pl.DeviceIdType.MESH,
        )

    loads = [
        pltpu.make_async_copy(source, target, load_sem.at[i])
        for i, (source, target) in enumerate(zip(far, held))
    ]
    for load in loads:
        load.start()

    lists_got[0:1] = jnp.zeros((1, 1, 128), jnp.int32)
    for x in range(2):
        for h in range(2):
            rows_got[x, h, 0:16, :] = jnp.zeros((16, quarter), BF)
        wide_got[x, 0:16, :] = jnp.zeros((16, half), BF)

    for load in loads[0:3]:
        load.wait()
    slots = jnp.concatenate([grid_list[...], mesh_list[...], dec_list[...]], axis=0).astype(F32)
    slots = jnp.concatenate([slots, jnp.zeros((N_DOM, 96), F32)], axis=1)
    slots = jnp.transpose(jnp.concatenate([slots, jnp.zeros((96, 128), F32)], axis=0))
    for p in range(N_DOM):
        lists_out[p] = slots[p : p + 1, :].astype(jnp.int32)

    pl.semaphore_wait(barrier, N_DOM - 1)
    for dz, dx in FAR_FIRST:
        send(
            lists_out.at[pl.ds(peer(dz, dx), 1)],
            lists_got.at[pl.ds(slot(-dz, -dx), 1)],
            lists_sem.at[0],
            lists_sem.at[1],
            (dz, dx),
        )

    for load in loads[3:6]:
        load.wait()
    grid_turned[:, channels - channels % 128 :] = jnp.zeros((n_grid, 128), BF)
    grid_turned[:, 0:channels] = jnp.transpose(grid_in[...])

    def embed(i, carry):
        part = pl.ds(pl.multiple_of(i * 512, 512), 512)
        latent = silu(dot(grid_turned[part, 0:channels], w_embed[...])).astype(BF)
        grid_latent[part, :] = latent
        enc_table[part, :] = dot(latent, w_grid_send[...]).astype(BF)
        return carry

    lax.fori_loop(0, n_grid // 512, embed, 0)

    def edge_rows(scratch, feat, sender, n_local, n_slots):
        value = sender[...]
        shifted = jnp.maximum(value - n_local, 0)
        giver = shifted >> (n_slots.bit_length() - 1)
        listed = shifted & (n_slots - 1)
        dz = ((giver >> 2) - me_z) & (N_Z - 1)
        dx = ((giver & (N_X - 1)) - me_x) & (N_X - 1)
        lent = ((listed >> 3) << 8) + ((dz * N_X + dx) << 3) + (listed & 7)
        local = value < n_local
        scratch[...] = jnp.zeros_like(scratch)
        scratch[0:4, :] = 0.5 * feat[...].astype(F32)
        scratch[4:5, :] = jnp.where(local, value, -1).astype(F32)
        scratch[5:6, :] = jnp.where(local, -1, lent).astype(F32)

    def sender_hot(scratch, hots, n_local, n_lent):
        def step(i, carry):
            part = pl.ds(pl.multiple_of(i * 128, 128), 128)
            turned = jnp.transpose(
                jnp.concatenate([scratch[:, part], jnp.zeros((120, 128), F32)], axis=0)
            )
            local = jnp.broadcast_to(turned[:, 4:5], (128, 128))
            lent = jnp.broadcast_to(turned[:, 5:6], (128, 128))
            for j in range(n_local // 128):
                hots[part, 128 * j : 128 * j + 128] = hot(local, 128.0 * j, 0.5)
            hots[part, n_local : n_local + 128] = turned.astype(BF)
            for j in range(n_lent // 128):
                at = n_local + 128 + 128 * j
                hots[part, at : at + 128] = hot(lent, 128.0 * j, 0.5)
            return carry

        lax.fori_loop(0, hots.shape[0] // 128, step, 0, unroll=8)

    def receiver_hot(target, hots, count):
        n_rows = hots.shape[0]
        count[...] = jnp.zeros_like(count)

        def step(i, carry):
            part = pl.ds(pl.multiple_of(i * 128, 128), 128)
            wanted = jnp.broadcast_to(target[:, part].astype(F32), (n_rows, 128))
            same = jnp.where(wanted == rows((n_rows, 128)), 1.0, 0.0)
            hots[:, part] = same.astype(BF)
            count[...] += same
            return carry

        lax.fori_loop(0, hots.shape[1] // 128, step, 0, unroll=4)
        total = jnp.sum(count[...], axis=1, keepdims=True)
        count[...] = jnp.broadcast_to(1.0 / jnp.maximum(total, 1.0), count.shape)

    def edge_weights(table, at, w_edge):
        table[at : at + 128, :] = jnp.zeros((128, width), BF)
        table[at : at + 4, :] = w_edge

    def mean(hots, messages, count):
        columns = messages.shape[1]
        return dot(hots, messages) * jnp.concatenate([count] * (columns // 128), axis=1)

    for load in loads[6:10]:
        load.wait()
    edge_rows(enc_rows, enc_feat, enc_sender, n_grid, SLOTS_GRID)
    sender_hot(enc_rows, enc_hot, n_grid, N_DOM * SLOTS_GRID)
    edge_weights(enc_table, n_grid, w_enc_edge[...])

    def ship(x, h):
        for dz, dx in FAR_FIRST:
            send(
                rows_out.at[x, h, pl.ds(16 * slot(dz, dx), 16)],
                rows_got.at[x, h, pl.ds(16 * slot(-dz, -dx), 16)],
                send_sem.at[4 * x + h],
                recv_sem.at[4 * x + h],
                (dz, dx),
            )

    def beside(values):
        columns = values.shape[1]
        got = values.astype(F32).reshape(N_DOM, 16, columns)
        low = got[:, 0:8, :].reshape(N_DOM * 8, columns)
        high = got[:, 8:16, :].reshape(N_DOM * 8, columns)
        return jnp.concatenate([low, high], axis=1).astype(BF)

    def arrive(x, h):
        wait_for(rows_got.at[x, h, pl.ds(16, 16 * (N_DOM - 1))], recv_sem.at[4 * x + h])
        return beside(rows_got[x, h])

    wait_for(lists_got.at[pl.ds(1, N_DOM - 1)], lists_sem.at[1])
    listed = lists_got[:, 0, :].astype(F32)
    listed = jnp.transpose(jnp.concatenate([listed, jnp.zeros((96, 128), F32)], axis=0))
    for h in range(2):
        for q in range(N_DOM):
            lend_grid[h, 8 * q : 8 * q + 8, :] = jnp.broadcast_to(
                listed[8 * h : 8 * h + 8, q : q + 1], (8, 128)
            )
        picks = jnp.concatenate(
            [hot(lend_grid[h], 128.0 * j) for j in range(n_grid // 128)], axis=1
        )
        lent = dot(picks, grid_turned[...]).reshape(N_DOM, 8, 2 * quarter)
        lent = jnp.concatenate([lent[:, :, 0:quarter], lent[:, :, quarter:]], axis=1)
        rows_out[0, h] = lent.reshape(16 * N_DOM, quarter).astype(BF)
        ship(0, h)

    for q in range(N_DOM):
        for lent, first in ((lend_mesh, 16), (lend_dec, 24)):
            column = jnp.broadcast_to(listed[first : first + 8, q : q + 1], (8, 128))
            lent[16 * q : 16 * q + 8, :] = column
            lent[16 * q + 8 : 16 * q + 16, :] = column + 128.0
    for k, lent in enumerate((lend_mesh, lend_dec)):
        lend_hot[k] = jnp.concatenate([hot(lent[...], 0.0), hot(lent[...], 128.0)], axis=1)

    def local_sums(hots, columns, table):
        def step(i, carry):
            part = pl.ds(pl.multiple_of(i * 1024, 1024), 1024)
            edge_sum[part, :] = dot(hots[part, 0:columns], table)
            return carry

        lax.fori_loop(0, hots.shape[0] // 1024, step, 0)

    local_sums(enc_hot, near, enc_table[...])
    receiver_hot(enc_offset, enc_to, enc_count)

    def embed_lent(h):
        latent = silu(dot(arrive(0, h)[:, 0:channels], w_embed[...])).astype(BF)
        enc_lent[...] = dot(latent, w_grid_send[...]).astype(BF)

    embed_lent(0)

    for i in range(enc_hot.shape[0] // 1024):
        part = pl.ds(i * 1024, 1024)
        edge_sum[part, :] += dot(enc_hot[part, near : near + 256], enc_lent[...])
    for load in loads[10:]:
        load.wait()
    embed_lent(1)

    summed = jnp.zeros((n_mesh, width), F32)
    for i in range(enc_hot.shape[0] // 1024):
        part = pl.ds(i * 1024, 1024)
        total = edge_sum[part, :] + dot(enc_hot[part, near + 256 :], enc_lent[...])
        summed += dot(enc_to[:, part], silu_of_half(total).astype(BF))
    mesh_now[...] = (summed * jnp.concatenate([enc_count[...]] * 4, axis=1)).astype(BF)

    def lend(x, h, picks, values):
        stacked = jnp.concatenate([values[:, 0:quarter], values[:, quarter:]], axis=0)
        rows_out[x, h] = dot(picks, stacked).astype(BF)
        ship(x, h)

    def messages_of(hots, table, h):
        at = h * half

        def step(i):
            part = pl.ds(i * 1024, 1024)
            total = edge_sum[part, at : at + half] + dot(hots[part, 256:512], table)
            message = silu_of_half(total).astype(BF)
            blocks = pl.ds(i * 8, 8)
            dec_msg[blocks, :, at : at + half] = message.reshape(8, 128, half)

        for i in range(hots.shape[0] // 1024):
            step(i)

    def sort_blocks():
        def rank_of(b, carry):
            own = dec_block[0, b] * 32 + b
            below = jnp.int32(0)
            for other in range(n_edge_blocks):
                below += jnp.where(dec_block[0, other] * 32 + other < own, 1, 0)
            rank[b] = below
            return carry

        lax.fori_loop(0, n_edge_blocks, rank_of, 0)

        def block_at(t, carry):
            found = jnp.int32(0)
            for b in range(n_edge_blocks):
                found += jnp.where(rank[b] == t, b, 0)
            order[t] = found
            return carry

        lax.fori_loop(0, n_edge_blocks, block_at, 0)

        def kept(t, carry):
            same = dec_block[0, order[t]] == dec_block[0, order[jnp.maximum(t - 1, 0)]]
            keep[t] = jnp.where(same, 1, 0)
            return carry

        lax.fori_loop(0, n_edge_blocks, kept, 0)

        def last_of(g, carry):
            before, until = jnp.int32(0), jnp.int32(0)
            for b in range(n_edge_blocks):
                before += jnp.where(dec_block[0, b] < g, 1, 0)
                until += jnp.where(dec_block[0, b] <= g, 1, 0)
            last[g] = jnp.where(until > before, until, 0)
            return carry

        lax.fori_loop(0, n_blocks, last_of, 0)

    def dec_receivers():
        def step(b, carry):
            part = pl.ds(pl.multiple_of(b * 128, 128), 128)
            wanted = jnp.broadcast_to(dec_offset[:, part].astype(F32), (128, 128))
            same = jnp.where(wanted == rows((128, 128)), 1.0, 0.0)
            dec_to[b] = same.astype(BF)
            block_count[b] = jnp.broadcast_to(
                jnp.sum(same, axis=1, keepdims=True), (128, 128)
            )
            return carry

        lax.fori_loop(0, n_edge_blocks, step, 0, unroll=4)
        total = jnp.zeros((128, 128), F32)
        running[0] = jnp.zeros((128, width), F32)
        for t in range(n_edge_blocks):
            total = block_count[order[t]] + keep[t].astype(F32) * total
            running[t + 1, :, 0:128] = total
        for g in range(n_blocks):
            count = running[last[g], :, 0:128]
            dec_count[128 * g : 128 * g + 128, :] = 1.0 / jnp.maximum(count, 1.0)

    for k in range(2):
        values = dot(mesh_now[...], w_proc_send[k]).astype(BF)
        stacked = jnp.concatenate([values[:, 0:half], values[:, half:]], axis=0)
        wide_out[k] = dot(lend_hot[0], stacked).astype(BF)
        for dz, dx in FAR_FIRST:
            send(
                wide_out.at[k, pl.ds(16 * slot(dz, dx), 16)],
                wide_got.at[k, pl.ds(16 * slot(-dz, -dx), 16)],
                send_sem.at[2 + k],
                recv_sem.at[2 + k],
                (dz, dx),
            )
        mesh_table[0:128, :] = values
        edge_weights(mesh_table, 128, w_proc_edge[k])
        if k == 0:
            edge_rows(mesh_rows, mesh_feat, mesh_sender, n_mesh, SLOTS_MESH)
            sender_hot(mesh_rows, mesh_hot, n_mesh, N_DOM * SLOTS_MESH)
            receiver_hot(mesh_offset, mesh_to, mesh_count)
            sort_blocks()
        local_sums(mesh_hot, 256, mesh_table[...])
        if k == 1:
            edge_rows(dec_rows, dec_feat, dec_sender, n_mesh, SLOTS_MESH)
            sender_hot(dec_rows, dec_hot, n_mesh, N_DOM * SLOTS_MESH)
            dec_receivers()
        wait_for(wide_got.at[k, pl.ds(16, 16 * (N_DOM - 1))], recv_sem.at[2 + k])
        total = edge_sum[0 : mesh_hot.shape[0], :] + dot(mesh_hot[:, 256:512], beside(wide_got[k]))
        message = silu_of_half(total).astype(BF)
        mesh_mean = mean(mesh_to[...], message, mesh_count[...]).astype(BF)
        update = silu(dot(mesh_mean, w_proc_node[k]))
        mesh_now[...] = (mesh_now[...].astype(F32) + update).astype(BF)

    for h in range(2):
        lend(1, h, lend_hot[1], mesh_now[:, h * half : h * half + half])
    mesh_table[0:128, :] = mesh_now[...]
    edge_weights(mesh_table, 128, w_dec_edge[...])
    local_sums(dec_hot, 256, mesh_table[...])
    mixed[...] = dot(grid_latent[...], w_skip[...])
    for h in range(2):
        at = h * half
        messages_of(dec_hot, arrive(1, h), h)
        total = jnp.zeros((128, half), F32)
        for t in range(n_edge_blocks):
            block = dot(dec_to[order[t]], dec_msg[order[t], :, at : at + half])
            total = block + keep[t].astype(F32) * total
            running[t + 1, :, at : at + half] = total
        for g in range(n_blocks):
            count = dec_count[128 * g : 128 * g + 128, :]
            grid_mean[128 * g : 128 * g + 128, :] = (
                running[last[g], :, at : at + half] * jnp.concatenate([count] * (half // 128), axis=1)
            ).astype(BF)
        total = mixed[...] + dot(grid_mean[...], w_dec[at : at + half, :])
        if h == 0:
            mixed[...] = total
        else:
            out[...] = dot_turned(w_out[...], silu(total).astype(BF)).astype(BF)

    wait_for(lists_got.at[pl.ds(1, N_DOM - 1)], lists_sem.at[0])
    for x in range(2):
        for h in range(2):
            wait_for(rows_out.at[x, h, pl.ds(16, 16 * (N_DOM - 1))], send_sem.at[4 * x + h])
        wait_for(wide_out.at[x, pl.ds(16, 16 * (N_DOM - 1))], send_sem.at[2 + x])


def local(
    grid_in,
    w_embed,
    w_grid_send,
    enc_feat,
    w_enc_edge,
    enc_sender,
    enc_offset,
    grid_rows,
    w_proc_send,
    w_proc_edge,
    w_proc_node,
    mesh_feat,
    mesh_sender,
    mesh_offset,
    mesh_rows,
    w_skip,
    w_dec,
    w_dec_edge,
    dec_feat,
    dec_sender,
    dec_offset,
    dec_block,
    dec_rows,
    w_out,
):
    n_grid = grid_in.shape[0]
    width = w_embed.shape[1]
    n_mesh = 128
    enc, mesh, dec = enc_sender.shape[0], mesh_sender.shape[0], dec_sender.shape[0]
    operands = (
        grid_rows.T,
        mesh_rows.T,
        dec_rows.T,
        grid_in.T,
        w_embed,
        w_grid_send,
        enc_sender.reshape(1, enc),
        enc_feat,
        w_enc_edge,
        enc_offset.reshape(1, enc),
        mesh_sender.reshape(1, mesh),
        mesh_feat,
        w_proc_edge,
        mesh_offset.reshape(1, mesh),
        w_proc_send,
        w_proc_node,
        dec_sender.reshape(1, dec),
        dec_feat,
        w_dec_edge,
        dec_offset.reshape(1, dec),
        dec_block.reshape(1, dec_block.shape[0]),
        w_skip,
        w_dec,
        w_out.T,
    )
    held = [
        pltpu.SMEM(operand.shape, operand.dtype)
        if i == 20
        else pltpu.VMEM(operand.shape, operand.dtype)
        for i, operand in enumerate(operands)
    ]
    most = max(enc, dec)
    forecast = pl.pallas_call(
        kernel,
        out_shape=pltpu.VMEM((w_out.shape[1], n_grid), BF),
        in_specs=[pl.BlockSpec(memory_space=pl.ANY)] * len(operands),
        out_specs=pl.BlockSpec(memory_space=pltpu.VMEM),
        scratch_shapes=held
        + [
            pltpu.VMEM((N_DOM, 1, 128), jnp.int32),
            pltpu.VMEM((N_DOM, 1, 128), jnp.int32),
            pltpu.VMEM((2, 2, 512, width // 4), BF),
            pltpu.VMEM((2, 2, 512, width // 4), BF),
            pltpu.VMEM((2, 512, width // 2), BF),
            pltpu.VMEM((2, 512, width // 2), BF),
            pltpu.VMEM((2, 256, 128), F32),
            pltpu.VMEM((512, 128), F32),
            pltpu.VMEM((512, 128), F32),
            pltpu.VMEM((2, 512, 256), BF),
            pltpu.VMEM((8, enc), F32),
            pltpu.VMEM((8, mesh), F32),
            pltpu.VMEM((8, dec), F32),
            pltpu.VMEM((enc, n_grid + 128 + 512), BF),
            pltpu.VMEM((mesh, 512), BF),
            pltpu.VMEM((dec, 512), BF),
            pltpu.VMEM((n_mesh, enc), BF),
            pltpu.VMEM((n_mesh, mesh), BF),
            pltpu.VMEM((dec // 128, 128, 128), BF),
            pltpu.VMEM((n_mesh, 128), F32),
            pltpu.VMEM((n_mesh, 128), F32),
            pltpu.VMEM((dec // 128, 128, 128), F32),
            pltpu.VMEM((n_grid, 128), F32),
            pltpu.VMEM((dec // 128 + 1, 128, width), F32),
            pltpu.VMEM((n_grid, 256), BF),
            pltpu.VMEM((n_grid, width), BF),
            pltpu.VMEM((n_grid + 128, width), BF),
            pltpu.VMEM((256, width), BF),
            pltpu.VMEM((256, width), BF),
            pltpu.VMEM((most, width), F32),
            pltpu.VMEM((dec // 128, 128, width), BF),
            pltpu.VMEM((n_mesh, width), BF),
            pltpu.VMEM((n_grid, width // 2), BF),
            pltpu.VMEM((n_grid, width), F32),
            pltpu.SMEM((dec // 128,), jnp.int32),
            pltpu.SMEM((dec // 128,), jnp.int32),
            pltpu.SMEM((dec // 128,), jnp.int32),
            pltpu.SMEM((n_grid // 128,), jnp.int32),
            pltpu.SemaphoreType.DMA((N_LOADS,)),
            pltpu.SemaphoreType.DMA((2,)),
            pltpu.SemaphoreType.DMA((6,)),
            pltpu.SemaphoreType.DMA((6,)),
        ],
        compiler_params=pltpu.CompilerParams(
            collective_id=0, has_side_effects=True, vmem_limit_bytes=56 * 1024 * 1024
        ),
        name="graph_weather",
    )(*operands)
    return forecast.T


def solution(mesh):
    in_specs = (
        P(("member", "dom"), None),
        P(),
        P(),
        P(None, "dom"),
        P(),
        P("dom"),
        P("dom"),
        P("dom", None),
        P(),
        P(),
        P(),
        P(None, "dom"),
        P("dom"),
        P("dom"),
        P("dom", None),
        P(),
        P(),
        P(),
        P(None, "dom"),
        P("dom"),
        P("dom"),
        P("dom"),
        P("dom", None),
        P(),
    )
    out_specs = P(("member", "dom"), None)
    return jax.shard_map(local, mesh=mesh, in_specs=in_specs, out_specs=out_specs, check_vma=False)
```

```python
import jax
import jax.numpy as jnp
from jax import lax
from jax.experimental import pallas as pl
from jax.experimental.pallas import tpu as pltpu
from jax.sharding import PartitionSpec as P

N_Z, N_X = 8, 4
N_DOM = N_Z * N_X
SLOTS_GRID = 16
SLOTS_MESH = 8
BF = jnp.bfloat16
F32 = jnp.float32
N_LOADS = 24


def silu_of_half(half):
    return half + half * jnp.tanh(half)


def silu(v):
    return silu_of_half(0.5 * v)


def dot(a, b):
    return jnp.dot(a, b, preferred_element_type=F32)


def dot_turned(a, b):
    return lax.dot_general(a, b, (((1,), (1,)), ((), ())), preferred_element_type=F32)


def lanes(shape):
    return lax.broadcasted_iota(jnp.int32, shape, 1).astype(F32)


def rows(shape):
    return lax.broadcasted_iota(jnp.int32, shape, 0).astype(F32)


def hot(index, offset, value=1.0):
    return jnp.where(index == lanes(index.shape) + offset, value, 0.0).astype(BF)


def hops(offset):
    dz, dx = offset
    return min(dz, N_Z - dz) + min(dx, N_X - dx)


OFFSETS = [(dz, dx) for dz in range(N_Z) for dx in range(N_X) if (dz, dx) != (0, 0)]
FAR_FIRST = sorted(OFFSETS, key=lambda offset: -hops(offset))


def slot(dz, dx):
    return (dz % N_Z) * N_X + dx % N_X


def kernel(*refs):
    far, out, held = refs[0:N_LOADS], refs[N_LOADS], refs[N_LOADS + 1 : 2 * N_LOADS + 1]
    (
        grid_list,
        mesh_list,
        dec_list,
        grid_in,
        w_embed,
        w_grid_send,
        enc_sender,
        enc_feat,
        w_enc_edge,
        enc_offset,
        mesh_sender,
        mesh_feat,
        w_proc_edge,
        mesh_offset,
        w_proc_send,
        w_proc_node,
        dec_sender,
        dec_feat,
        w_dec_edge,
        dec_offset,
        dec_block,
        w_skip,
        w_dec,
        w_out,
    ) = held
    (
        lists_out,
        lists_got,
        rows_out,
        rows_got,
        wide_out,
        wide_got,
        lend_grid,
        lend_mesh,
        lend_dec,
        lend_hot,
        enc_rows,
        mesh_rows,
        dec_rows,
        enc_hot,
        mesh_hot,
        dec_hot,
        enc_to,
        mesh_to,
        dec_to,
        enc_count,
        mesh_count,
        block_count,
        dec_count,
        running,
        grid_turned,
        grid_latent,
        enc_table,
        enc_lent,
        mesh_table,
        edge_sum,
        dec_msg,
        mesh_now,
        grid_mean,
        mixed,
        rank,
        order,
        keep,
        last,
        load_sem,
        lists_sem,
        send_sem,
        recv_sem,
    ) = refs[2 * N_LOADS + 1 :]
    me = lax.axis_index("dom")
    me_z, me_x = me // N_X, lax.rem(me, N_X)
    width = w_embed.shape[1]
    half = width // 2
    quarter = width // 4
    channels, n_grid = grid_in.shape
    n_mesh = mesh_to.shape[0]
    n_edge_blocks = dec_block.shape[1]
    n_blocks = n_grid // 128
    near = n_grid + 128

    def peer(dz, dx):
        return lax.rem(me_z + dz, N_Z) * N_X + lax.rem(me_x + dx, N_X)

    def send(source, target, out_sem, in_sem, offset):
        pltpu.make_async_remote_copy(
            src_ref=source,
            dst_ref=target,
            send_sem=out_sem,
            recv_sem=in_sem,
            device_id={"dom": peer(*offset)},
            device_id_type=pl.DeviceIdType.MESH,
        ).start()

    def wait_for(part, sem):
        pltpu.make_async_copy(part, part, sem).wait()

    barrier = pltpu.get_barrier_semaphore()
    for offset in FAR_FIRST:
        pl.semaphore_signal(
            barrier,
            inc=1,
            device_id={"dom": peer(*offset)},
            device_id_type=pl.DeviceIdType.MESH,
        )

    loads = [
        pltpu.make_async_copy(source, target, load_sem.at[i])
        for i, (source, target) in enumerate(zip(far, held))
    ]
    for load in loads:
        load.start()

    lists_got[0:1] = jnp.zeros((1, 1, 128), jnp.int32)
    for x in range(2):
        for h in range(2):
            rows_got[x, h, 0:16, :] = jnp.zeros((16, quarter), BF)
        wide_got[x, 0:16, :] = jnp.zeros((16, half), BF)

    for load in loads[0:3]:
        load.wait()
    slots = jnp.concatenate([grid_list[...], mesh_list[...], dec_list[...]], axis=0).astype(F32)
    slots = jnp.concatenate([slots, jnp.zeros((N_DOM, 96), F32)], axis=1)
    slots = jnp.transpose(jnp.concatenate([slots, jnp.zeros((96, 128), F32)], axis=0))
    for p in range(N_DOM):
        lists_out[p] = slots[p : p + 1, :].astype(jnp.int32)

    pl.semaphore_wait(barrier, N_DOM - 1)
    for dz, dx in FAR_FIRST:
        send(
            lists_out.at[pl.ds(peer(dz, dx), 1)],
            lists_got.at[pl.ds(slot(-dz, -dx), 1)],
            lists_sem.at[0],
            lists_sem.at[1],
            (dz, dx),
        )

    for load in loads[3:6]:
        load.wait()
    grid_turned[:, channels - channels % 128 :] = jnp.zeros((n_grid, 128), BF)
    grid_turned[:, 0:channels] = jnp.transpose(grid_in[...])

    def embed(i, carry):
        part = pl.ds(i * 512, 512)
        latent = silu(dot(grid_turned[part, 0:channels], w_embed[...])).astype(BF)
        grid_latent[part, :] = latent
        enc_table[part, :] = dot(latent, w_grid_send[...]).astype(BF)
        return carry

    for i in range(n_grid // 512):
        embed(i, 0)

    def edge_rows(scratch, feat, sender, n_local, n_slots):
        value = sender[...]
        shifted = jnp.maximum(value - n_local, 0)
        giver = shifted >> (n_slots.bit_length() - 1)
        listed = shifted & (n_slots - 1)
        dz = ((giver >> 2) - me_z) & (N_Z - 1)
        dx = ((giver & (N_X - 1)) - me_x) & (N_X - 1)
        lent = ((listed >> 3) << 8) + ((dz * N_X + dx) << 3) + (listed & 7)
        local = value < n_local
        scratch[...] = jnp.zeros_like(scratch)
        scratch[0:4, :] = 0.5 * feat[...].astype(F32)
        scratch[4:5, :] = jnp.where(local, value, -1).astype(F32)
        scratch[5:6, :] = jnp.where(local, -1, lent).astype(F32)

    def sender_hot(scratch, hots, n_local, n_lent, first=0, last=None):
        def step(i, carry):
            part = pl.ds(pl.multiple_of(i * 128, 128), 128)
            turned = jnp.transpose(
                jnp.concatenate([scratch[:, part], jnp.zeros((120, 128), F32)], axis=0)
            )
            local = jnp.broadcast_to(turned[:, 4:5], (128, 128))
            lent = jnp.broadcast_to(turned[:, 5:6], (128, 128))
            for j in range(n_local // 128):
                hots[part, 128 * j : 128 * j + 128] = hot(local, 128.0 * j, 0.5)
            hots[part, n_local : n_local + 128] = turned.astype(BF)
            for j in range(n_lent // 128):
                at = n_local + 128 + 128 * j
                hots[part, at : at + 128] = hot(lent, 128.0 * j, 0.5)
            return carry

        last = hots.shape[0] // 128 if last is None else last
        lax.fori_loop(first, last, step, 0, unroll=8)

    def receiver_hot(target, hots, count):
        n_rows = hots.shape[0]
        count[...] = jnp.zeros_like(count)

        def step(i, carry):
            part = pl.ds(pl.multiple_of(i * 128, 128), 128)
            wanted = jnp.broadcast_to(target[:, part].astype(F32), (n_rows, 128))
            same = jnp.where(wanted == rows((n_rows, 128)), 1.0, 0.0)
            hots[:, part] = same.astype(BF)
            count[...] += same
            return carry

        lax.fori_loop(0, hots.shape[1] // 128, step, 0, unroll=4)
        total = jnp.sum(count[...], axis=1, keepdims=True)
        count[...] = jnp.broadcast_to(1.0 / jnp.maximum(total, 1.0), count.shape)

    def edge_weights(table, at, w_edge):
        table[at : at + 128, :] = jnp.zeros((128, width), BF)
        table[at : at + 4, :] = w_edge

    def mean(hots, messages, count):
        columns = messages.shape[1]
        return dot(hots, messages) * jnp.concatenate([count] * (columns // 128), axis=1)

    for load in loads[6:10]:
        load.wait()
    edge_rows(enc_rows, enc_feat, enc_sender, n_grid, SLOTS_GRID)
    sender_hot(enc_rows, enc_hot, n_grid, N_DOM * SLOTS_GRID, 0, 8)
    edge_weights(enc_table, n_grid, w_enc_edge[...])

    def ship(x, h):
        for dz, dx in FAR_FIRST:
            send(
                rows_out.at[x, h, pl.ds(16 * slot(dz, dx), 16)],
                rows_got.at[x, h, pl.ds(16 * slot(-dz, -dx), 16)],
                send_sem.at[4 * x + h],
                recv_sem.at[4 * x + h],
                (dz, dx),
            )

    def beside(values):
        columns = values.shape[1]
        got = values.astype(F32).reshape(N_DOM, 16, columns)
        low = got[:, 0:8, :].reshape(N_DOM * 8, columns)
        high = got[:, 8:16, :].reshape(N_DOM * 8, columns)
        return jnp.concatenate([low, high], axis=1).astype(BF)

    def arrive(x, h):
        wait_for(rows_got.at[x, h, pl.ds(16, 16 * (N_DOM - 1))], recv_sem.at[4 * x + h])
        return beside(rows_got[x, h])

    wait_for(lists_got.at[pl.ds(1, N_DOM - 1)], lists_sem.at[1])
    listed = lists_got[:, 0, :].astype(F32)
    listed = jnp.transpose(jnp.concatenate([listed, jnp.zeros((96, 128), F32)], axis=0))
    for h in range(2):
        for q in range(N_DOM):
            lend_grid[h, 8 * q : 8 * q + 8, :] = jnp.broadcast_to(
                listed[8 * h : 8 * h + 8, q : q + 1], (8, 128)
            )
        picks = jnp.concatenate(
            [hot(lend_grid[h], 128.0 * j) for j in range(n_grid // 128)], axis=1
        )
        lent = dot(picks, grid_turned[...]).reshape(N_DOM, 8, 2 * quarter)
        lent = jnp.concatenate([lent[:, :, 0:quarter], lent[:, :, quarter:]], axis=1)
        rows_out[0, h] = lent.reshape(16 * N_DOM, quarter).astype(BF)
        ship(0, h)

    def mesh_lend(k, lent, first):
        for q in range(N_DOM):
            column = jnp.broadcast_to(listed[first : first + 8, q : q + 1], (8, 128))
            lent[16 * q : 16 * q + 8, :] = column
            lent[16 * q + 8 : 16 * q + 16, :] = column + 128.0
        lend_hot[k] = jnp.concatenate([hot(lent[...], 0.0), hot(lent[...], 128.0)], axis=1)

    mesh_lend(0, lend_mesh, 16)

    def local_sums(hots, columns, table):
        def step(i, carry):
            part = pl.ds(pl.multiple_of(i * 1024, 1024), 1024)
            edge_sum[part, :] = dot(hots[part, 0:columns], table)
            return carry

        lax.fori_loop(0, hots.shape[0] // 1024, step, 0)

    sender_hot(enc_rows, enc_hot, n_grid, N_DOM * SLOTS_GRID, 8, 16)
    local_sums(enc_hot, near, enc_table[...])
    receiver_hot(enc_offset, enc_to, enc_count)

    def embed_lent(h):
        latent = silu(dot(arrive(0, h)[:, 0:channels], w_embed[...])).astype(BF)
        enc_lent[...] = dot(latent, w_grid_send[...]).astype(BF)

    embed_lent(0)

    for i in range(enc_hot.shape[0] // 1024):
        part = pl.ds(i * 1024, 1024)
        edge_sum[part, :] += dot(enc_hot[part, near : near + 256], enc_lent[...])
    for load in loads[10:]:
        load.wait()
    embed_lent(1)

    summed = jnp.zeros((n_mesh, width), F32)
    for i in range(enc_hot.shape[0] // 1024):
        part = pl.ds(i * 1024, 1024)
        total = edge_sum[part, :] + dot(enc_hot[part, near + 256 :], enc_lent[...])
        summed += dot(enc_to[:, part], silu_of_half(total).astype(BF))
    mesh_now[...] = (summed * jnp.concatenate([enc_count[...]] * 4, axis=1)).astype(BF)

    def lend(x, h, picks, values):
        stacked = jnp.concatenate([values[:, 0:quarter], values[:, quarter:]], axis=0)
        rows_out[x, h] = dot(picks, stacked).astype(BF)
        ship(x, h)

    def messages_of(hots, table, h):
        at = h * half

        def step(i):
            part = pl.ds(i * 1024, 1024)
            total = edge_sum[part, at : at + half] + dot(hots[part, 256:512], table)
            message = silu_of_half(total).astype(BF)
            blocks = pl.ds(i * 8, 8)
            dec_msg[blocks, :, at : at + half] = message.reshape(8, 128, half)

        for i in range(hots.shape[0] // 1024):
            step(i)

    def sort_blocks():
        def rank_of(b, carry):
            own = dec_block[0, b] * 32 + b
            below = jnp.int32(0)
            for other in range(n_edge_blocks):
                below += jnp.where(dec_block[0, other] * 32 + other < own, 1, 0)
            rank[b] = below
            return carry

        lax.fori_loop(0, n_edge_blocks, rank_of, 0)

        def block_at(t, carry):
            found = jnp.int32(0)
            for b in range(n_edge_blocks):
                found += jnp.where(rank[b] == t, b, 0)
            order[t] = found
            return carry

        lax.fori_loop(0, n_edge_blocks, block_at, 0)

        def kept(t, carry):
            same = dec_block[0, order[t]] == dec_block[0, order[jnp.maximum(t - 1, 0)]]
            keep[t] = jnp.where(same, 1, 0)
            return carry

        lax.fori_loop(0, n_edge_blocks, kept, 0)

        def last_of(g, carry):
            before, until = jnp.int32(0), jnp.int32(0)
            for b in range(n_edge_blocks):
                before += jnp.where(dec_block[0, b] < g, 1, 0)
                until += jnp.where(dec_block[0, b] <= g, 1, 0)
            last[g] = jnp.where(until > before, until, 0)
            return carry

        lax.fori_loop(0, n_blocks, last_of, 0)

    def dec_receivers():
        def step(b, carry):
            part = pl.ds(pl.multiple_of(b * 128, 128), 128)
            wanted = jnp.broadcast_to(dec_offset[:, part].astype(F32), (128, 128))
            same = jnp.where(wanted == rows((128, 128)), 1.0, 0.0)
            dec_to[b] = same.astype(BF)
            block_count[b] = jnp.broadcast_to(
                jnp.sum(same, axis=1, keepdims=True), (128, 128)
            )
            return carry

        lax.fori_loop(0, n_edge_blocks, step, 0, unroll=4)
        total = jnp.zeros((128, 128), F32)
        running[0] = jnp.zeros((128, width), F32)
        for t in range(n_edge_blocks):
            total = block_count[order[t]] + keep[t].astype(F32) * total
            running[t + 1, :, 0:128] = total
        for g in range(n_blocks):
            count = running[last[g], :, 0:128]
            dec_count[128 * g : 128 * g + 128, :] = 1.0 / jnp.maximum(count, 1.0)

    for k in range(2):
        values = dot(mesh_now[...], w_proc_send[k]).astype(BF)
        stacked = jnp.concatenate([values[:, 0:half], values[:, half:]], axis=0)
        wide_out[k] = dot(lend_hot[0], stacked).astype(BF)
        for dz, dx in FAR_FIRST:
            send(
                wide_out.at[k, pl.ds(16 * slot(dz, dx), 16)],
                wide_got.at[k, pl.ds(16 * slot(-dz, -dx), 16)],
                send_sem.at[2 + k],
                recv_sem.at[2 + k],
                (dz, dx),
            )
        mesh_table[0:128, :] = values
        edge_weights(mesh_table, 128, w_proc_edge[k])
        if k == 0:
            edge_rows(mesh_rows, mesh_feat, mesh_sender, n_mesh, SLOTS_MESH)
            sender_hot(mesh_rows, mesh_hot, n_mesh, N_DOM * SLOTS_MESH)
            receiver_hot(mesh_offset, mesh_to, mesh_count)
            sort_blocks()
        local_sums(mesh_hot, 256, mesh_table[...])
        if k == 1:
            edge_rows(dec_rows, dec_feat, dec_sender, n_mesh, SLOTS_MESH)
            sender_hot(dec_rows, dec_hot, n_mesh, N_DOM * SLOTS_MESH)
            dec_receivers()
            mesh_lend(1, lend_dec, 24)
        wait_for(wide_got.at[k, pl.ds(16, 16 * (N_DOM - 1))], recv_sem.at[2 + k])
        total = edge_sum[0 : mesh_hot.shape[0], :] + dot(mesh_hot[:, 256:512], beside(wide_got[k]))
        message = silu_of_half(total).astype(BF)
        mesh_mean = mean(mesh_to[...], message, mesh_count[...]).astype(BF)
        update = silu(dot(mesh_mean, w_proc_node[k]))
        mesh_now[...] = (mesh_now[...].astype(F32) + update).astype(BF)

    for h in range(2):
        lend(1, h, lend_hot[1], mesh_now[:, h * half : h * half + half])
    mesh_table[0:128, :] = mesh_now[...]
    edge_weights(mesh_table, 128, w_dec_edge[...])
    local_sums(dec_hot, 256, mesh_table[...])
    mixed[...] = dot(grid_latent[...], w_skip[...])
    for h in range(2):
        at = h * half
        messages_of(dec_hot, arrive(1, h), h)
        total = jnp.zeros((128, half), F32)
        for t in range(n_edge_blocks):
            block = dot(dec_to[order[t]], dec_msg[order[t], :, at : at + half])
            total = block + keep[t].astype(F32) * total
            running[t + 1, :, at : at + half] = total
        for g in range(n_blocks):
            count = dec_count[128 * g : 128 * g + 128, :]
            grid_mean[128 * g : 128 * g + 128, :] = (
                running[last[g], :, at : at + half] * jnp.concatenate([count] * (half // 128), axis=1)
            ).astype(BF)
        for i in range(n_grid // 512):
            part = pl.ds(512 * i, 512)
            total = mixed[part, :] + dot(grid_mean[part, :], w_dec[at : at + half, :])
            if h == 0:
                mixed[part, :] = total
            else:
                out[:, part] = dot_turned(w_out[...], silu(total).astype(BF)).astype(BF)

    wait_for(lists_got.at[pl.ds(1, N_DOM - 1)], lists_sem.at[0])
    for x in range(2):
        for h in range(2):
            wait_for(rows_out.at[x, h, pl.ds(16, 16 * (N_DOM - 1))], send_sem.at[4 * x + h])
        wait_for(wide_out.at[x, pl.ds(16, 16 * (N_DOM - 1))], send_sem.at[2 + x])


def local(
    grid_in,
    w_embed,
    w_grid_send,
    enc_feat,
    w_enc_edge,
    enc_sender,
    enc_offset,
    grid_rows,
    w_proc_send,
    w_proc_edge,
    w_proc_node,
    mesh_feat,
    mesh_sender,
    mesh_offset,
    mesh_rows,
    w_skip,
    w_dec,
    w_dec_edge,
    dec_feat,
    dec_sender,
    dec_offset,
    dec_block,
    dec_rows,
    w_out,
):
    n_grid = grid_in.shape[0]
    width = w_embed.shape[1]
    n_mesh = 128
    enc, mesh, dec = enc_sender.shape[0], mesh_sender.shape[0], dec_sender.shape[0]
    operands = (
        grid_rows.T,
        mesh_rows.T,
        dec_rows.T,
        grid_in.T,
        w_embed,
        w_grid_send,
        enc_sender.reshape(1, enc),
        enc_feat,
        w_enc_edge,
        enc_offset.reshape(1, enc),
        mesh_sender.reshape(1, mesh),
        mesh_feat,
        w_proc_edge,
        mesh_offset.reshape(1, mesh),
        w_proc_send,
        w_proc_node,
        dec_sender.reshape(1, dec),
        dec_feat,
        w_dec_edge,
        dec_offset.reshape(1, dec),
        dec_block.reshape(1, dec_block.shape[0]),
        w_skip,
        w_dec,
        w_out.T,
    )
    held = [
        pltpu.SMEM(operand.shape, operand.dtype)
        if i == 20
        else pltpu.VMEM(operand.shape, operand.dtype)
        for i, operand in enumerate(operands)
    ]
    most = max(enc, dec)
    forecast = pl.pallas_call(
        kernel,
        out_shape=pltpu.VMEM((w_out.shape[1], n_grid), BF),
        in_specs=[pl.BlockSpec(memory_space=pl.ANY)] * len(operands),
        out_specs=pl.BlockSpec(memory_space=pltpu.VMEM),
        scratch_shapes=held
        + [
            pltpu.VMEM((N_DOM, 1, 128), jnp.int32),
            pltpu.VMEM((N_DOM, 1, 128), jnp.int32),
            pltpu.VMEM((2, 2, 512, width // 4), BF),
            pltpu.VMEM((2, 2, 512, width // 4), BF),
            pltpu.VMEM((2, 512, width // 2), BF),
            pltpu.VMEM((2, 512, width // 2), BF),
            pltpu.VMEM((2, 256, 128), F32),
            pltpu.VMEM((512, 128), F32),
            pltpu.VMEM((512, 128), F32),
            pltpu.VMEM((2, 512, 256), BF),
            pltpu.VMEM((8, enc), F32),
            pltpu.VMEM((8, mesh), F32),
            pltpu.VMEM((8, dec), F32),
            pltpu.VMEM((enc, n_grid + 128 + 512), BF),
            pltpu.VMEM((mesh, 512), BF),
            pltpu.VMEM((dec, 512), BF),
            pltpu.VMEM((n_mesh, enc), BF),
            pltpu.VMEM((n_mesh, mesh), BF),
            pltpu.VMEM((dec // 128, 128, 128), BF),
            pltpu.VMEM((n_mesh, 128), F32),
            pltpu.VMEM((n_mesh, 128), F32),
            pltpu.VMEM((dec // 128, 128, 128), F32),
            pltpu.VMEM((n_grid, 128), F32),
            pltpu.VMEM((dec // 128 + 1, 128, width), F32),
            pltpu.VMEM((n_grid, 256), BF),
            pltpu.VMEM((n_grid, width), BF),
            pltpu.VMEM((n_grid + 128, width), BF),
            pltpu.VMEM((256, width), BF),
            pltpu.VMEM((256, width), BF),
            pltpu.VMEM((most, width), F32),
            pltpu.VMEM((dec // 128, 128, width), BF),
            pltpu.VMEM((n_mesh, width), BF),
            pltpu.VMEM((n_grid, width // 2), BF),
            pltpu.VMEM((n_grid, width), F32),
            pltpu.SMEM((dec // 128,), jnp.int32),
            pltpu.SMEM((dec // 128,), jnp.int32),
            pltpu.SMEM((dec // 128,), jnp.int32),
            pltpu.SMEM((n_grid // 128,), jnp.int32),
            pltpu.SemaphoreType.DMA((N_LOADS,)),
            pltpu.SemaphoreType.DMA((2,)),
            pltpu.SemaphoreType.DMA((6,)),
            pltpu.SemaphoreType.DMA((6,)),
        ],
        compiler_params=pltpu.CompilerParams(
            collective_id=0, has_side_effects=True, vmem_limit_bytes=56 * 1024 * 1024
        ),
        name="graph_weather",
    )(*operands)
    return forecast.T


def solution(mesh):
    in_specs = (
        P(("member", "dom"), None),
        P(),
        P(),
        P(None, "dom"),
        P(),
        P("dom"),
        P("dom"),
        P("dom", None),
        P(),
        P(),
        P(),
        P(None, "dom"),
        P("dom"),
        P("dom"),
        P("dom", None),
        P(),
        P(),
        P(),
        P(None, "dom"),
        P("dom"),
        P("dom"),
        P("dom"),
        P("dom", None),
        P(),
    )
    out_specs = P(("member", "dom"), None)
    return jax.shard_map(local, mesh=mesh, in_specs=in_specs, out_specs=out_specs, check_vma=False)
```

```python
import jax
import jax.numpy as jnp
from jax import lax
from jax.experimental import pallas as pl
from jax.experimental.pallas import tpu as pltpu
from jax.sharding import PartitionSpec as P

N_Z, N_X = 8, 4
N_DOM = N_Z * N_X
SLOTS_GRID = 16
SLOTS_MESH = 8
BF = jnp.bfloat16
F32 = jnp.float32
N_LOADS = 24


def silu_of_half(half):
    return half + half * jnp.tanh(half)


def silu(v):
    return silu_of_half(0.5 * v)


def dot(a, b):
    return jnp.dot(a, b, preferred_element_type=F32)


def dot_turned(a, b):
    return lax.dot_general(a, b, (((1,), (1,)), ((), ())), preferred_element_type=F32)


def lanes(shape):
    return lax.broadcasted_iota(jnp.int32, shape, 1).astype(F32)


def rows(shape):
    return lax.broadcasted_iota(jnp.int32, shape, 0).astype(F32)


def hot(index, offset, value=1.0):
    return jnp.where(index == lanes(index.shape) + offset, value, 0.0).astype(BF)


def hops(offset):
    dz, dx = offset
    return min(dz, N_Z - dz) + min(dx, N_X - dx)


OFFSETS = [(dz, dx) for dz in range(N_Z) for dx in range(N_X) if (dz, dx) != (0, 0)]
FAR_FIRST = sorted(OFFSETS, key=lambda offset: -hops(offset))


def slot(dz, dx):
    return (dz % N_Z) * N_X + dx % N_X


def kernel(*refs):
    far, out, held = refs[0:N_LOADS], refs[N_LOADS], refs[N_LOADS + 1 : 2 * N_LOADS + 1]
    (
        grid_list,
        mesh_list,
        dec_list,
        grid_in,
        w_embed,
        w_grid_send,
        enc_sender,
        enc_feat,
        w_enc_edge,
        enc_offset,
        mesh_sender,
        mesh_feat,
        w_proc_edge,
        mesh_offset,
        w_proc_send,
        w_proc_node,
        dec_sender,
        dec_feat,
        w_dec_edge,
        dec_offset,
        dec_block,
        w_skip,
        w_dec,
        w_out,
    ) = held
    (
        lists_out,
        lists_got,
        rows_out,
        rows_got,
        wide_out,
        wide_got,
        lend_grid,
        lend_mesh,
        lend_dec,
        lend_hot,
        enc_rows,
        mesh_rows,
        dec_rows,
        enc_hot,
        mesh_hot,
        dec_hot,
        enc_to,
        mesh_to,
        dec_to,
        enc_count,
        mesh_count,
        block_count,
        dec_count,
        running,
        grid_turned,
        grid_latent,
        enc_table,
        enc_lent,
        mesh_table,
        edge_sum,
        dec_msg,
        mesh_now,
        grid_mean,
        mixed,
        rank,
        order,
        keep,
        last,
        load_sem,
        lists_sem,
        send_sem,
        recv_sem,
    ) = refs[2 * N_LOADS + 1 :]
    me = lax.axis_index("dom")
    me_z, me_x = me // N_X, lax.rem(me, N_X)
    width = w_embed.shape[1]
    half = width // 2
    quarter = width // 4
    channels, n_grid = grid_in.shape
    n_mesh = mesh_to.shape[0]
    n_edge_blocks = dec_block.shape[1]
    n_blocks = n_grid // 128
    near = n_grid + 128

    def peer(dz, dx):
        return lax.rem(me_z + dz, N_Z) * N_X + lax.rem(me_x + dx, N_X)

    def send(source, target, out_sem, in_sem, offset):
        pltpu.make_async_remote_copy(
            src_ref=source,
            dst_ref=target,
            send_sem=out_sem,
            recv_sem=in_sem,
            device_id={"dom": peer(*offset)},
            device_id_type=pl.DeviceIdType.MESH,
        ).start()

    def wait_for(part, sem):
        pltpu.make_async_copy(part, part, sem).wait()

    barrier = pltpu.get_barrier_semaphore()
    for offset in FAR_FIRST:
        pl.semaphore_signal(
            barrier,
            inc=1,
            device_id={"dom": peer(*offset)},
            device_id_type=pl.DeviceIdType.MESH,
        )

    loads = [
        pltpu.make_async_copy(source, target, load_sem.at[i])
        for i, (source, target) in enumerate(zip(far, held))
    ]
    for load in loads:
        load.start()

    lists_got[0:1] = jnp.zeros((1, 1, 128), jnp.int32)
    for x in range(2):
        for h in range(2):
            rows_got[x, h, 0:16, :] = jnp.zeros((16, quarter), BF)
        wide_got[x, 0:16, :] = jnp.zeros((16, half), BF)

    for load in loads[0:3]:
        load.wait()
    slots = jnp.concatenate([grid_list[...], mesh_list[...], dec_list[...]], axis=0).astype(F32)
    slots = jnp.concatenate([slots, jnp.zeros((N_DOM, 96), F32)], axis=1)
    slots = jnp.transpose(jnp.concatenate([slots, jnp.zeros((96, 128), F32)], axis=0))
    for p in range(N_DOM):
        lists_out[p] = slots[p : p + 1, :].astype(jnp.int32)

    pl.semaphore_wait(barrier, N_DOM - 1)
    for dz, dx in FAR_FIRST:
        send(
            lists_out.at[pl.ds(peer(dz, dx), 1)],
            lists_got.at[pl.ds(slot(-dz, -dx), 1)],
            lists_sem.at[0],
            lists_sem.at[1],
            (dz, dx),
        )

    for load in loads[3:6]:
        load.wait()
    grid_turned[:, channels - channels % 128 :] = jnp.zeros((n_grid, 128), BF)
    grid_turned[:, 0:channels] = jnp.transpose(grid_in[...])

    def embed(i, carry):
        part = pl.ds(i * 512, 512)
        latent = silu(dot(grid_turned[part, 0:channels], w_embed[...])).astype(BF)
        grid_latent[part, :] = latent
        enc_table[part, :] = dot(latent, w_grid_send[...]).astype(BF)
        return carry

    for i in range(n_grid // 512):
        embed(i, 0)

    def edge_rows(scratch, feat, sender, n_local, n_slots):
        value = sender[...]
        shifted = jnp.maximum(value - n_local, 0)
        giver = shifted >> (n_slots.bit_length() - 1)
        listed = shifted & (n_slots - 1)
        dz = ((giver >> 2) - me_z) & (N_Z - 1)
        dx = ((giver & (N_X - 1)) - me_x) & (N_X - 1)
        lent = ((listed >> 3) << 8) + ((dz * N_X + dx) << 3) + (listed & 7)
        local = value < n_local
        scratch[...] = jnp.zeros_like(scratch)
        scratch[0:4, :] = 0.5 * feat[...].astype(F32)
        scratch[4:5, :] = jnp.where(local, value, -1).astype(F32)
        scratch[5:6, :] = jnp.where(local, -1, lent).astype(F32)

    def sender_hot(scratch, hots, n_local, n_lent, first=0, last=None):
        def step(i, carry):
            part = pl.ds(pl.multiple_of(i * 128, 128), 128)
            turned = jnp.transpose(
                jnp.concatenate([scratch[:, part], jnp.zeros((120, 128), F32)], axis=0)
            )
            local = jnp.broadcast_to(turned[:, 4:5], (128, 128))
            lent = jnp.broadcast_to(turned[:, 5:6], (128, 128))
            for j in range(n_local // 128):
                hots[part, 128 * j : 128 * j + 128] = hot(local, 128.0 * j, 0.5)
            hots[part, n_local : n_local + 128] = turned.astype(BF)
            for j in range(n_lent // 128):
                at = n_local + 128 + 128 * j
                hots[part, at : at + 128] = hot(lent, 128.0 * j, 0.5)
            return carry

        last = hots.shape[0] // 128 if last is None else last
        lax.fori_loop(first, last, step, 0, unroll=8)

    def receiver_hot(target, hots, count):
        n_rows = hots.shape[0]
        count[...] = jnp.zeros_like(count)

        def step(i, carry):
            part = pl.ds(pl.multiple_of(i * 128, 128), 128)
            wanted = jnp.broadcast_to(target[:, part].astype(F32), (n_rows, 128))
            same = jnp.where(wanted == rows((n_rows, 128)), 1.0, 0.0)
            hots[:, part] = same.astype(BF)
            count[...] += same
            return carry

        lax.fori_loop(0, hots.shape[1] // 128, step, 0, unroll=4)
        total = jnp.sum(count[...], axis=1, keepdims=True)
        count[...] = jnp.broadcast_to(1.0 / jnp.maximum(total, 1.0), count.shape)

    def edge_weights(table, at, w_edge):
        table[at : at + 128, :] = jnp.zeros((128, width), BF)
        table[at : at + 4, :] = w_edge

    def mean(hots, messages, count):
        columns = messages.shape[1]
        return dot(hots, messages) * jnp.concatenate([count] * (columns // 128), axis=1)

    for load in loads[6:10]:
        load.wait()
    edge_rows(enc_rows, enc_feat, enc_sender, n_grid, SLOTS_GRID)
    sender_hot(enc_rows, enc_hot, n_grid, N_DOM * SLOTS_GRID, 0, 8)
    edge_weights(enc_table, n_grid, w_enc_edge[...])

    def ship(x, h):
        for dz, dx in FAR_FIRST:
            send(
                rows_out.at[x, h, pl.ds(16 * slot(dz, dx), 16)],
                rows_got.at[x, h, pl.ds(16 * slot(-dz, -dx), 16)],
                send_sem.at[4 * x + h],
                recv_sem.at[4 * x + h],
                (dz, dx),
            )

    def beside(values):
        columns = values.shape[1]
        got = values.astype(F32).reshape(N_DOM, 16, columns)
        low = got[:, 0:8, :].reshape(N_DOM * 8, columns)
        high = got[:, 8:16, :].reshape(N_DOM * 8, columns)
        return jnp.concatenate([low, high], axis=1).astype(BF)

    def arrive(x, h):
        wait_for(rows_got.at[x, h, pl.ds(16, 16 * (N_DOM - 1))], recv_sem.at[4 * x + h])
        return beside(rows_got[x, h])

    wait_for(lists_got.at[pl.ds(1, N_DOM - 1)], lists_sem.at[1])
    listed = lists_got[:, 0, :].astype(F32)
    listed = jnp.transpose(jnp.concatenate([listed, jnp.zeros((96, 128), F32)], axis=0))
    for h in range(2):
        for q in range(N_DOM):
            lend_grid[h, 8 * q : 8 * q + 8, :] = jnp.broadcast_to(
                listed[8 * h : 8 * h + 8, q : q + 1], (8, 128)
            )
        picks = jnp.concatenate(
            [hot(lend_grid[h], 128.0 * j) for j in range(n_grid // 128)], axis=1
        )
        lent = dot(picks, grid_turned[...]).reshape(N_DOM, 8, 2 * quarter)
        lent = jnp.concatenate([lent[:, :, 0:quarter], lent[:, :, quarter:]], axis=1)
        rows_out[0, h] = lent.reshape(16 * N_DOM, quarter).astype(BF)
        ship(0, h)

    def mesh_lend(k, lent, first):
        for q in range(N_DOM):
            column = jnp.broadcast_to(listed[first : first + 8, q : q + 1], (8, 128))
            lent[16 * q : 16 * q + 8, :] = column
            lent[16 * q + 8 : 16 * q + 16, :] = column + 128.0
        lend_hot[k] = jnp.concatenate([hot(lent[...], 0.0), hot(lent[...], 128.0)], axis=1)

    mesh_lend(0, lend_mesh, 16)

    def local_sums(hots, columns, table):
        for i in range(hots.shape[0] // 1024):
            part = pl.ds(i * 1024, 1024)
            edge_sum[part, :] = dot(hots[part, 0:columns], table)

    sender_hot(enc_rows, enc_hot, n_grid, N_DOM * SLOTS_GRID, 8, 16)
    local_sums(enc_hot, near, enc_table[...])
    receiver_hot(enc_offset, enc_to, enc_count)

    def embed_lent(h):
        latent = silu(dot(arrive(0, h)[:, 0:channels], w_embed[...])).astype(BF)
        enc_lent[...] = dot(latent, w_grid_send[...]).astype(BF)

    embed_lent(0)

    for i in range(enc_hot.shape[0] // 1024):
        part = pl.ds(i * 1024, 1024)
        edge_sum[part, :] += dot(enc_hot[part, near : near + 256], enc_lent[...])
    for load in loads[10:]:
        load.wait()
    embed_lent(1)

    summed = jnp.zeros((n_mesh, width), F32)
    for i in range(enc_hot.shape[0] // 1024):
        part = pl.ds(i * 1024, 1024)
        total = edge_sum[part, :] + dot(enc_hot[part, near + 256 :], enc_lent[...])
        summed += dot(enc_to[:, part], silu_of_half(total).astype(BF))
    mesh_now[...] = (summed * jnp.concatenate([enc_count[...]] * 4, axis=1)).astype(BF)

    def lend(x, h, picks, values):
        stacked = jnp.concatenate([values[:, 0:quarter], values[:, quarter:]], axis=0)
        rows_out[x, h] = dot(picks, stacked).astype(BF)
        ship(x, h)

    def messages_of(hots, table, h):
        at = h * half

        def step(i):
            part = pl.ds(i * 1024, 1024)
            total = edge_sum[part, at : at + half] + dot(hots[part, 256:512], table)
            message = silu_of_half(total).astype(BF)
            blocks = pl.ds(i * 8, 8)
            dec_msg[blocks, :, at : at + half] = message.reshape(8, 128, half)

        for i in range(hots.shape[0] // 1024):
            step(i)

    def sort_blocks():
        def rank_of(b, carry):
            own = dec_block[0, b] * 32 + b
            below = jnp.int32(0)
            for other in range(n_edge_blocks):
                below += jnp.where(dec_block[0, other] * 32 + other < own, 1, 0)
            rank[b] = below
            return carry

        lax.fori_loop(0, n_edge_blocks, rank_of, 0)

        def block_at(t, carry):
            found = jnp.int32(0)
            for b in range(n_edge_blocks):
                found += jnp.where(rank[b] == t, b, 0)
            order[t] = found
            return carry

        lax.fori_loop(0, n_edge_blocks, block_at, 0)

        def kept(t, carry):
            same = dec_block[0, order[t]] == dec_block[0, order[jnp.maximum(t - 1, 0)]]
            keep[t] = jnp.where(same, 1, 0)
            return carry

        lax.fori_loop(0, n_edge_blocks, kept, 0)

        def last_of(g, carry):
            before, until = jnp.int32(0), jnp.int32(0)
            for b in range(n_edge_blocks):
                before += jnp.where(dec_block[0, b] < g, 1, 0)
                until += jnp.where(dec_block[0, b] <= g, 1, 0)
            last[g] = jnp.where(until > before, until, 0)
            return carry

        lax.fori_loop(0, n_blocks, last_of, 0)

    def dec_receivers():
        def step(b, carry):
            part = pl.ds(pl.multiple_of(b * 128, 128), 128)
            wanted = jnp.broadcast_to(dec_offset[:, part].astype(F32), (128, 128))
            same = jnp.where(wanted == rows((128, 128)), 1.0, 0.0)
            dec_to[b] = same.astype(BF)
            block_count[b] = jnp.broadcast_to(
                jnp.sum(same, axis=1, keepdims=True), (128, 128)
            )
            return carry

        lax.fori_loop(0, n_edge_blocks, step, 0, unroll=4)
        total = jnp.zeros((128, 128), F32)
        running[0] = jnp.zeros((128, width), F32)
        for t in range(n_edge_blocks):
            total = block_count[order[t]] + keep[t].astype(F32) * total
            running[t + 1, :, 0:128] = total
        for g in range(n_blocks):
            count = running[last[g], :, 0:128]
            dec_count[128 * g : 128 * g + 128, :] = 1.0 / jnp.maximum(count, 1.0)

    for k in range(2):
        values = dot(mesh_now[...], w_proc_send[k]).astype(BF)
        stacked = jnp.concatenate([values[:, 0:half], values[:, half:]], axis=0)
        wide_out[k] = dot(lend_hot[0], stacked).astype(BF)
        for dz, dx in FAR_FIRST:
            send(
                wide_out.at[k, pl.ds(16 * slot(dz, dx), 16)],
                wide_got.at[k, pl.ds(16 * slot(-dz, -dx), 16)],
                send_sem.at[2 + k],
                recv_sem.at[2 + k],
                (dz, dx),
            )
        mesh_table[0:128, :] = values
        edge_weights(mesh_table, 128, w_proc_edge[k])
        if k == 0:
            edge_rows(mesh_rows, mesh_feat, mesh_sender, n_mesh, SLOTS_MESH)
            sender_hot(mesh_rows, mesh_hot, n_mesh, N_DOM * SLOTS_MESH)
            receiver_hot(mesh_offset, mesh_to, mesh_count)
            sort_blocks()
        local_sums(mesh_hot, 256, mesh_table[...])
        if k == 1:
            edge_rows(dec_rows, dec_feat, dec_sender, n_mesh, SLOTS_MESH)
            sender_hot(dec_rows, dec_hot, n_mesh, N_DOM * SLOTS_MESH)
            dec_receivers()
            mesh_lend(1, lend_dec, 24)
        wait_for(wide_got.at[k, pl.ds(16, 16 * (N_DOM - 1))], recv_sem.at[2 + k])
        total = edge_sum[0 : mesh_hot.shape[0], :] + dot(mesh_hot[:, 256:512], beside(wide_got[k]))
        message = silu_of_half(total).astype(BF)
        mesh_mean = mean(mesh_to[...], message, mesh_count[...]).astype(BF)
        update = silu(dot(mesh_mean, w_proc_node[k]))
        mesh_now[...] = (mesh_now[...].astype(F32) + update).astype(BF)

    for h in range(2):
        lend(1, h, lend_hot[1], mesh_now[:, h * half : h * half + half])
    mesh_table[0:128, :] = mesh_now[...]
    edge_weights(mesh_table, 128, w_dec_edge[...])
    local_sums(dec_hot, 256, mesh_table[...])
    mixed[...] = dot(grid_latent[...], w_skip[...])
    for h in range(2):
        at = h * half
        messages_of(dec_hot, arrive(1, h), h)
        total = jnp.zeros((128, half), F32)
        for t in range(n_edge_blocks):
            block = dot(dec_to[order[t]], dec_msg[order[t], :, at : at + half])
            total = block + keep[t].astype(F32) * total
            running[t + 1, :, at : at + half] = total
        for g in range(n_blocks):
            count = dec_count[128 * g : 128 * g + 128, :]
            grid_mean[128 * g : 128 * g + 128, :] = (
                running[last[g], :, at : at + half] * jnp.concatenate([count] * (half // 128), axis=1)
            ).astype(BF)
        for i in range(n_grid // 512):
            part = pl.ds(512 * i, 512)
            total = mixed[part, :] + dot(grid_mean[part, :], w_dec[at : at + half, :])
            if h == 0:
                mixed[part, :] = total
            else:
                out[:, part] = dot_turned(w_out[...], silu(total).astype(BF)).astype(BF)

    wait_for(lists_got.at[pl.ds(1, N_DOM - 1)], lists_sem.at[0])
    for x in range(2):
        for h in range(2):
            wait_for(rows_out.at[x, h, pl.ds(16, 16 * (N_DOM - 1))], send_sem.at[4 * x + h])
        wait_for(wide_out.at[x, pl.ds(16, 16 * (N_DOM - 1))], send_sem.at[2 + x])


def local(
    grid_in,
    w_embed,
    w_grid_send,
    enc_feat,
    w_enc_edge,
    enc_sender,
    enc_offset,
    grid_rows,
    w_proc_send,
    w_proc_edge,
    w_proc_node,
    mesh_feat,
    mesh_sender,
    mesh_offset,
    mesh_rows,
    w_skip,
    w_dec,
    w_dec_edge,
    dec_feat,
    dec_sender,
    dec_offset,
    dec_block,
    dec_rows,
    w_out,
):
    n_grid = grid_in.shape[0]
    width = w_embed.shape[1]
    n_mesh = 128
    enc, mesh, dec = enc_sender.shape[0], mesh_sender.shape[0], dec_sender.shape[0]
    operands = (
        grid_rows.T,
        mesh_rows.T,
        dec_rows.T,
        grid_in.T,
        w_embed,
        w_grid_send,
        enc_sender.reshape(1, enc),
        enc_feat,
        w_enc_edge,
        enc_offset.reshape(1, enc),
        mesh_sender.reshape(1, mesh),
        mesh_feat,
        w_proc_edge,
        mesh_offset.reshape(1, mesh),
        w_proc_send,
        w_proc_node,
        dec_sender.reshape(1, dec),
        dec_feat,
        w_dec_edge,
        dec_offset.reshape(1, dec),
        dec_block.reshape(1, dec_block.shape[0]),
        w_skip,
        w_dec,
        w_out.T,
    )
    held = [
        pltpu.SMEM(operand.shape, operand.dtype)
        if i == 20
        else pltpu.VMEM(operand.shape, operand.dtype)
        for i, operand in enumerate(operands)
    ]
    most = max(enc, dec)
    forecast = pl.pallas_call(
        kernel,
        out_shape=pltpu.VMEM((w_out.shape[1], n_grid), BF),
        in_specs=[pl.BlockSpec(memory_space=pl.ANY)] * len(operands),
        out_specs=pl.BlockSpec(memory_space=pltpu.VMEM),
        scratch_shapes=held
        + [
            pltpu.VMEM((N_DOM, 1, 128), jnp.int32),
            pltpu.VMEM((N_DOM, 1, 128), jnp.int32),
            pltpu.VMEM((2, 2, 512, width // 4), BF),
            pltpu.VMEM((2, 2, 512, width // 4), BF),
            pltpu.VMEM((2, 512, width // 2), BF),
            pltpu.VMEM((2, 512, width // 2), BF),
            pltpu.VMEM((2, 256, 128), F32),
            pltpu.VMEM((512, 128), F32),
            pltpu.VMEM((512, 128), F32),
            pltpu.VMEM((2, 512, 256), BF),
            pltpu.VMEM((8, enc), F32),
            pltpu.VMEM((8, mesh), F32),
            pltpu.VMEM((8, dec), F32),
            pltpu.VMEM((enc, n_grid + 128 + 512), BF),
            pltpu.VMEM((mesh, 512), BF),
            pltpu.VMEM((dec, 512), BF),
            pltpu.VMEM((n_mesh, enc), BF),
            pltpu.VMEM((n_mesh, mesh), BF),
            pltpu.VMEM((dec // 128, 128, 128), BF),
            pltpu.VMEM((n_mesh, 128), F32),
            pltpu.VMEM((n_mesh, 128), F32),
            pltpu.VMEM((dec // 128, 128, 128), F32),
            pltpu.VMEM((n_grid, 128), F32),
            pltpu.VMEM((dec // 128 + 1, 128, width), F32),
            pltpu.VMEM((n_grid, 256), BF),
            pltpu.VMEM((n_grid, width), BF),
            pltpu.VMEM((n_grid + 128, width), BF),
            pltpu.VMEM((256, width), BF),
            pltpu.VMEM((256, width), BF),
            pltpu.VMEM((most, width), F32),
            pltpu.VMEM((dec // 128, 128, width), BF),
            pltpu.VMEM((n_mesh, width), BF),
            pltpu.VMEM((n_grid, width // 2), BF),
            pltpu.VMEM((n_grid, width), F32),
            pltpu.SMEM((dec // 128,), jnp.int32),
            pltpu.SMEM((dec // 128,), jnp.int32),
            pltpu.SMEM((dec // 128,), jnp.int32),
            pltpu.SMEM((n_grid // 128,), jnp.int32),
            pltpu.SemaphoreType.DMA((N_LOADS,)),
            pltpu.SemaphoreType.DMA((2,)),
            pltpu.SemaphoreType.DMA((6,)),
            pltpu.SemaphoreType.DMA((6,)),
        ],
        compiler_params=pltpu.CompilerParams(
            collective_id=0, has_side_effects=True, vmem_limit_bytes=56 * 1024 * 1024
        ),
        name="graph_weather",
    )(*operands)
    return forecast.T


def solution(mesh):
    in_specs = (
        P(("member", "dom"), None),
        P(),
        P(),
        P(None, "dom"),
        P(),
        P("dom"),
        P("dom"),
        P("dom", None),
        P(),
        P(),
        P(),
        P(None, "dom"),
        P("dom"),
        P("dom"),
        P("dom", None),
        P(),
        P(),
        P(),
        P(None, "dom"),
        P("dom"),
        P("dom"),
        P("dom"),
        P("dom", None),
        P(),
    )
    out_specs = P(("member", "dom"), None)
    return jax.shard_map(local, mesh=mesh, in_specs=in_specs, out_specs=out_specs, check_vma=False)
```
